256 devices in a mesh: ctx: 64 (over y, x_hi, z), head: 4 (over x_lo, core).
Axes of the slice: x: 4 (x_hi: 2, x_lo: 2; x = x_hi * 2 + x_lo), y: 4, z: 8, core: 2. Of those that a mesh axis runs over, the one named last changes fastest.
Arguments:
- query_all: bfloat16 [8192, 1024], P('ctx', 'head'), may hold values from -6 to 6
- key_all: bfloat16 [8192, 1024], P('ctx', 'head'), may hold values from -6 to 6
- value_all: bfloat16 [8192, 1024], P('ctx', 'head'), may hold values from -6 to 6
- cotangent: bfloat16 [8192, 1024], P('ctx', 'head'), may hold values from -16 to 16
- conv_input: bfloat16 [8192, 1024], P('ctx', 'head'), may hold values from -6 to 6
- rec_lengths: int32 [3], replicated, may hold values from 1365 to 2730
- out_proj: bfloat16 [1024, 1024], P(None, 'head'), may hold values from -0.1875 to 0.1875
- conv_weight: bfloat16 [31, 1024], P(None, 'head'), may hold values from -1 to 1
Outputs:
- q_grad: bfloat16 [8192, 1024], P('ctx', 'head')
- k_grad: bfloat16 [8192, 1024], P('ctx', 'head')
- v_grad: bfloat16 [8192, 1024], P('ctx', 'head')
- x_grad: bfloat16 [8192, 1024], P('ctx', 'head')
- out_proj_grad: float32 [1024, 1024], P('ctx', 'head')
- conv_weight_grad: float32 [31, 1024], P(None, 'head')
The draws below stay inside these ranges and needn't reach their ends.
Inputs may be any that keep to these rules, and one draw needn't show every extreme that they name: `rec_lengths`: the recordings lie end to end from frame 0; frames from their total on are padding.
All inputs are finite; a program needn't handle non-finite values.
Results may differ from the reference program's by a relative error of at most 0.03.
Values may be sent and summed in bfloat16 or wider, within the bound.
A program may use at most 64 MiB of HBM per device.

```python
import math
import jax
import jax.numpy as jnp
from jax import lax

HEADS = 16
HEAD_DIM = 64
D = 1024
KW = 31
NREC = 3
FRAMES = 8192


def draw_query_all(key, part):
    values = jnp.clip(1.4 * jax.random.normal(jax.random.fold_in(key, 11), (FRAMES, D), jnp.float32), -6.0, 6.0)
    return values.astype(jnp.bfloat16)


def draw_key_all(key, part):
    values = jnp.clip(1.4 * jax.random.normal(jax.random.fold_in(key, 23), (FRAMES, D), jnp.float32), -6.0, 6.0)
    return values.astype(jnp.bfloat16)


def strengthened(entries, own_key, source, target, shards_of, factor):
    def block_of(dim):
        return (jnp.arange(entries.shape[dim]) // (entries.shape[dim] // shards_of)).reshape((-1,) + (1,) * (entries.ndim - 1 - dim))

    near = jax.random.permutation(own_key, shards_of)[block_of(target)]
    other_side = (block_of(target) + shards_of // 2) % shards_of
    return jnp.where((block_of(source) == near) | (block_of(source) == other_side), factor * entries, entries)


def level_of(key, shape, split, low, high):
    level, own = 1.0, jax.random.fold_in(key, 6)
    for position, parts in split:
        draws = jnp.exp(jax.random.uniform(jax.random.fold_in(own, position), (parts,), jnp.float32, low / len(split), high / len(split)))
        level = level * jnp.repeat(draws, shape[position] // parts).reshape([-1 if axis == position else 1 for axis in range(len(shape))])
    return level


def gaussian(rng, extent, width, most, cuts=(), kind=jnp.bfloat16):
    values = width * jax.random.normal(rng, extent, jnp.float32)
    if cuts:
        values = values * level_of(rng, extent, cuts, -0.22, 0.18)
    return jnp.clip(values, -most, most).astype(kind)


def noise_with(stream_key, extent, scale, most, shards, heavy, kind=jnp.bfloat16):
    array = scale * jax.random.normal(stream_key, extent, jnp.float32)
    if shards:
        array = array * level_of(stream_key, extent, shards, -0.22, 0.18)
    return jnp.clip(strengthened(array, jax.random.fold_in(stream_key, 3), *heavy), -most, most).astype(kind)


def setup_inputs(seed: int = 0) -> dict:
    keys = jax.random.split(jax.random.key(seed), 9)
    query_all = draw_query_all(jax.random.fold_in(keys[8], 71), 0)
    key_all = draw_key_all(jax.random.fold_in(keys[8], 71), 0)
    value_all = gaussian(keys[2], (FRAMES, D), 1.0, 6.0, ((0, 64), (1, 4)))
    cotangent = noise_with(keys[3], (FRAMES, D), 1.0, 16.0, ((0, 64), (1, 4)), (0, 1, 64, 4.0))
    conv_input = gaussian(keys[4], (FRAMES, D), 1.0, 6.0, ((0, 64), (1, 4)))
    rec_lengths = jax.random.randint(keys[5], (NREC,), FRAMES // 6, FRAMES // 3 + 1).astype(jnp.int32)
    out_proj = gaussian(keys[6], (D, D), D ** -0.5, 0.1875, ((1, 4),))
    conv_weight = gaussian(keys[7], (KW, D), KW ** -0.5, 1.0, ((1, 4),))
    return {"query_all": query_all, "key_all": key_all, "value_all": value_all, "cotangent": cotangent, "conv_input": conv_input, "rec_lengths": rec_lengths, "out_proj": out_proj, "conv_weight": conv_weight}


def conv_forward(extended, taps, frames):
    wide = extended.astype(jnp.float32)
    weights = taps.astype(jnp.float32)
    result = jnp.zeros((frames, extended.shape[1]), jnp.float32)
    for offset in range(taps.shape[0]):
        result = result + weights[offset] * wide[offset:offset + frames]
    return result


def conv_backward(grad_ext, taps, frames):
    wide = grad_ext.astype(jnp.float32)
    weights = taps.astype(jnp.float32)
    reach = taps.shape[0] - 1
    result = jnp.zeros((frames, grad_ext.shape[1]), jnp.float32)
    for offset in range(taps.shape[0]):
        result = result + weights[offset] * wide[reach - offset:reach - offset + frames]
    return result


def tap_products(grad_conv, extended):
    frames = grad_conv.shape[0]
    wide = extended.astype(jnp.float32)
    grad_wide = grad_conv.astype(jnp.float32)
    rows_out = [jnp.sum(grad_wide * wide[offset:offset + frames], axis=0) for offset in range(extended.shape[0] - frames + 1)]
    return jnp.stack(rows_out)


def gate_slope(conv_out, upstream):
    sigmoid_value = jax.nn.sigmoid(conv_out)
    return (upstream.astype(jnp.float32) * sigmoid_value * (1.0 + conv_out * (1.0 - sigmoid_value))).astype(jnp.bfloat16)


def reference(query_all, key_all, value_all, cotangent, conv_input, rec_lengths, out_proj, conv_weight):
    half_taps = KW // 2
    score_scale = HEAD_DIM ** -0.5
    valid_total = jnp.sum(rec_lengths)
    positions = jnp.arange(FRAMES, dtype=jnp.int32)
    frame_ok = positions < valid_total
    masked = jnp.where(frame_ok[:, None], conv_input, jnp.zeros_like(conv_input))
    padded_input = jnp.pad(masked, ((half_taps, half_taps), (0, 0)))
    conv_out = conv_forward(padded_input, conv_weight, FRAMES)
    grad_conv = gate_slope(conv_out, cotangent)
    conv_weight_grad = tap_products(grad_conv, padded_input)
    padded_grad = jnp.pad(grad_conv, ((half_taps, half_taps), (0, 0)))
    grad_input = conv_backward(padded_grad, conv_weight, FRAMES)
    x_grad = (cotangent.astype(jnp.float32) + jnp.where(frame_ok[:, None], grad_input, 0.0)).astype(jnp.bfloat16)
    grad_out = jnp.dot(x_grad, out_proj, preferred_element_type=jnp.float32).astype(jnp.bfloat16)

    def per_head(matrix):
        return jnp.transpose(matrix.reshape(FRAMES, HEADS, HEAD_DIM), (1, 0, 2))

    block_rows = math.gcd(FRAMES, 512)
    block_count = FRAMES // block_rows

    def one_head(operands):
        query_head, key_head, value_head, grad_head = operands
        keys32 = key_head.astype(jnp.float32)

        def query_block(running, block_index):
            key_acc, value_acc = running
            first_row = (block_index * block_rows).astype(jnp.int32)
            query_rows = lax.dynamic_slice_in_dim(query_head, first_row, block_rows, 0)
            grad_rows = lax.dynamic_slice_in_dim(grad_head, first_row, block_rows, 0)
            scores = jnp.dot(query_rows, key_head.T, preferred_element_type=jnp.float32) * score_scale
            scores = jnp.where(frame_ok[None, :], scores, -jnp.inf)
            row_max = jnp.max(scores, axis=-1)
            totals = jnp.sum(jnp.exp(scores - row_max[:, None]), axis=-1)
            log_total = row_max + jnp.log(totals)
            probs = jnp.exp(scores - log_total[:, None])
            probs16 = probs.astype(jnp.bfloat16)
            attn_out = jnp.dot(probs16, value_head, preferred_element_type=jnp.float32)
            delta = jnp.sum(grad_rows.astype(jnp.float32) * attn_out, axis=-1)
            slopes = jnp.dot(grad_rows, value_head.T, preferred_element_type=jnp.float32)
            dscores = probs * (slopes - delta[:, None])
            dscores16 = dscores.astype(jnp.bfloat16)
            query_grad = score_scale * jnp.dot(dscores, keys32, precision=lax.Precision.HIGHEST)
            key_acc = key_acc + jnp.dot(dscores16.T, query_rows, preferred_element_type=jnp.float32)
            value_acc = value_acc + jnp.dot(probs16.T, grad_rows, preferred_element_type=jnp.float32)
            return (key_acc, value_acc), (query_grad, attn_out)

        zeros_head = jnp.zeros((FRAMES, HEAD_DIM), jnp.float32)
        sums, blocks_out = lax.scan(query_block, (zeros_head, zeros_head), jnp.arange(block_count, dtype=jnp.int32))
        query_grad = blocks_out[0].reshape(FRAMES, HEAD_DIM)
        attn_out = blocks_out[1].reshape(FRAMES, HEAD_DIM)
        return query_grad, score_scale * sums[0], sums[1], attn_out

    results = lax.map(one_head, (per_head(query_all), per_head(key_all), per_head(value_all), per_head(grad_out)))

    def join_heads(tensor):
        return jnp.transpose(tensor, (1, 0, 2)).reshape(FRAMES, HEADS * HEAD_DIM)

    q_grad = join_heads(results[0]).astype(jnp.bfloat16)
    k_grad = join_heads(results[1]).astype(jnp.bfloat16)
    v_grad = join_heads(results[2]).astype(jnp.bfloat16)
    attn16 = join_heads(results[3]).astype(jnp.bfloat16)
    out_proj_grad = jnp.dot(x_grad.T, attn16, preferred_element_type=jnp.float32)
    return (q_grad, k_grad, v_grad, x_grad, out_proj_grad, conv_weight_grad)
```

```python
import functools

import jax
import jax.numpy as jnp
from jax import lax
from jax.experimental import pallas as pl
from jax.experimental.pallas import tpu as pltpu
from jax.sharding import PartitionSpec as P

F32, BF16 = jnp.float32, jnp.bfloat16
HEAD_DIM = 64
ROWS = 128
WIDTH = 256
PAIR = 128
BLOCK = 256
TAPS = 31
NEG = -1e30
LOG2E = 1.4426950408889634
MESH = pl.DeviceIdType.MESH


def nt(a, b):
    return lax.dot_general(a, b, (((1,), (1,)), ((), ())), preferred_element_type=F32)


def tn(a, b):
    return lax.dot_general(a, b, (((0,), (0,)), ((), ())), preferred_element_type=F32)


def nn(a, b):
    return jnp.dot(a, b, preferred_element_type=F32)


def iota(shape, dim):
    return lax.broadcasted_iota(jnp.int32, shape, dim)


def fused_kernel(
    Y, Z,
    rec, q, k, v, ct, ci, w, taps,
    q_o, k_o, v_o, x_o, g_o, c_o,
    kv, qg, dog, kt, va, ka, vta, qta, probs, mk, mrun, ot, dot_, dqt, mst, lin, dlt, gbuf, dsb,
    hci, hct, ext, gex, xf, do_s,
    st, os, orr, of, ox, gs, gr, gy, gx, gt, gz, gzr,
    acc, rss, rsr, fk, dqs, dqr, fq,
    cwp, cwr, c1, cx, cz, cfin,
    halo_s, halo_r, head_s, head_r, xs, xr, ys, yr, kvs, kvr, rs_s, rs_r, gzs, gzrs, czs, czr,
):
    Q = Y * BLOCK
    N = 2 * Y * Z
    ctx, head = lax.axis_index("ctx"), lax.axis_index("head")
    y = lax.div(ctx, 2 * Z)
    xh = lax.rem(lax.div(ctx, Z), 2)
    z = lax.rem(ctx, Z)
    other = 1 - xh

    def at(yy, xx, zz):
        return ((yy * 2 + xx) * Z + zz, head)

    def y_peer(d):
        return at(lax.rem(y + d, Y), xh, z)

    def z_peer(d):
        return at(y, xh, lax.rem(z + d, Z))

    def head_peer(d):
        return (ctx, lax.rem(head + d, Y))

    partner = at(y, other, z)
    following = (lax.rem(ctx + 1, N), head)
    preceding = (lax.rem(ctx + N - 1, N), head)

    def remote(src, dst, send, recv, device):
        return pltpu.make_async_remote_copy(
            src_ref=src, dst_ref=dst, send_sem=send, recv_sem=recv, device_id=device, device_id_type=MESH
        )

    own_cols = pl.ds(pl.multiple_of(xh * PAIR, PAIR), PAIR)
    other_cols = pl.ds(pl.multiple_of(other * PAIR, PAIR), PAIR)

    def halo(i):
        src, dst, dev = (
            (ci.at[pl.ds(ROWS - 32, 32)], hci.at[0], following),
            (ci.at[pl.ds(0, 32)], hci.at[1], preceding),
            (ct.at[pl.ds(ROWS - 16, 16)], hct.at[0], following),
            (ct.at[pl.ds(0, 16)], hct.at[1], preceding),
        )[i]
        return remote(src, dst, halo_s.at[i], halo_r.at[i], dev)

    XK, XV, XQ, XDO, XO, XG, XDK, XDV, XDQ, XCW = range(10)

    def x_copy(i):
        src, dst = (
            lambda: (k.at[:, other_cols], kv.at[0, 0, xh]),
            lambda: (v.at[:, other_cols], kv.at[0, 1, xh]),
            lambda: (q.at[:, other_cols], qg.at[0, xh]),
            lambda: (do_s.at[:, other_cols], dog.at[0, xh]),
            lambda: (of.at[other], ox),
            lambda: (gy.at[other], gx),
            lambda: (fk.at[0, other], k_o.at[:, own_cols]),
            lambda: (fk.at[1, other], v_o.at[:, own_cols]),
            lambda: (fq.at[other], q_o.at[:, own_cols]),
            lambda: (c1, cx),
        )[i]()
        return remote(src, dst, xs.at[i], xr.at[i], partner)

    YQ, YDO, YST, YO, YG, YDQ, YC1, YC2 = range(8)

    def y_copy(i, d):
        src, dst = (
            lambda: (qg.at[0], qg.at[d]),
            lambda: (dog.at[0], dog.at[d]),
            lambda: (st.at[0], st.at[d]),
            lambda: (os.at[Y - d], orr.at[d]),
            lambda: (gs.at[lax.rem(y + d, Y)], gr.at[d]),
            lambda: (dqs.at[Y - d], dqr.at[d]),
            lambda: (cwp.at[lax.rem(y + d, Y)], cwr.at[d]),
            lambda: (cfin.at[y], cfin.at[y]),
        )[i]()
        return remote(src, dst, ys.at[i, d], yr.at[i, d], y_peer(d))

    def y_start(i):
        for d in range(1, Y):
            y_copy(i, d).start()

    def y_recv(i):
        for d in range(1, Y):
            y_copy(i, d).wait_recv()

    def kv_copy(slot):
        if isinstance(slot, int):
            up = slot <= Z // 2
            src, dev = (slot - 1, z_peer(1)) if up else ((slot + 1) % Z, z_peer(Z - 1))
            return remote(kv.at[src], kv.at[slot], kvs.at[slot], kvr.at[slot], dev)
        raise ValueError

    def rs_copy(s, dev):
        return remote(rss.at[s], rsr.at[s], rs_s.at[s], rs_r.at[s], dev)

    def gz_copy(d):
        return remote(gz.at[lax.rem(z + d, Z)], gzr.at[d], gzs.at[d], gzrs.at[d], z_peer(d))

    def cz_copy(d):
        return remote(cz.at[z], cz.at[z], czs.at[d], czr.at[d], z_peer(d))

    peers = [partner, following, preceding]
    peers += [y_peer(d) for d in range(1, Y)] + [z_peer(d) for d in range(1, Z)]
    peers += [head_peer(d) for d in range(1, Y)]
    barrier = pltpu.get_barrier_semaphore()
    for peer in peers:
        pl.semaphore_signal(barrier, inc=1, device_id=peer, device_id_type=MESH)
    pl.semaphore_wait(barrier, len(peers))

    for i in range(4):
        halo(i).start()
    for i in (XK, XV, XQ):
        x_copy(i).start()
    kv[0, 0, pl.ds(xh, 1)] = k[:, own_cols][None]
    kv[0, 1, pl.ds(xh, 1)] = v[:, own_cols][None]
    qg[0, pl.ds(xh, 1)] = q[:, own_cols][None]
    valid = rec[0] + rec[1] + rec[2]

    for i in (0, 1):
        halo(i).wait_recv()
    pos = ctx * ROWS - 32 + iota((ROWS + 64, WIDTH), 0)
    ext[...] = jnp.where(
        (pos >= 0) & (pos < valid), jnp.concatenate([hci[0], ci[...], hci[1]], axis=0).astype(F32), 0.0
    )
    for i in (2, 3):
        halo(i).wait_recv()
    weights = taps[...].astype(F32)
    for c in range(2):
        cols = slice(c * 128, c * 128 + 128)
        conv = jnp.zeros((ROWS + 32, 128), F32)
        for b in range(8):
            moved = ext[b : b + ROWS + 56, cols]
            for a in range(4):
                j = 8 * a + b - 1
                if 0 <= j < TAPS:
                    conv = conv + weights[j : j + 1, cols] * moved[8 * a : 8 * a + ROWS + 32]
        sig = jax.nn.sigmoid(conv)
        up = jnp.concatenate([hct[0, :, cols], ct[:, cols], hct[1, :, cols]], axis=0).astype(F32)
        slope = (up * sig * (1.0 + conv * (1.0 - sig))).astype(BF16).astype(F32)
        gpos = ctx * ROWS - 16 + iota((ROWS + 32, 128), 0)
        gex[:, cols] = jnp.where((gpos >= 0) & (gpos < N * ROWS), slope, 0.0)

    for i in (XK, XV):
        x_copy(i).wait_recv()
    kv_copy(1).start()
    kv_copy(Z - 1).start()
    x_copy(XQ).wait_recv()
    y_start(YQ)

    for c in range(2):
        cols = slice(c * 128, c * 128 + 128)
        back = jnp.zeros((ROWS, 128), F32)
        for b in range(8):
            moved = gex[b : b + ROWS + 24, cols]
            for a in range(4):
                j = TAPS - 8 * a - b
                if 0 <= j < TAPS:
                    back = back + weights[j : j + 1, cols] * moved[8 * a : 8 * a + ROWS]
        frame = ctx * ROWS + iota((ROWS, 128), 0)
        x16 = (ct[:, cols].astype(F32) + jnp.where(frame < valid, back, 0.0)).astype(BF16)
        x_o[:, cols] = x16
        xf[pl.ds(head, 1), :, cols] = x16[None]

    def head_copy(d, slot):
        return remote(xf.at[slot], xf.at[slot], head_s.at[d], head_r.at[d], head_peer(d))

    for d in range(1, Y):
        head_copy(d, head).start()

    crow = 32 // Y
    for c in range(2):
        cols = slice(c * 128, c * 128 + 128)
        grad = gex[16 : 16 + ROWS, cols]
        for b in range(8):
            moved = ext[b : b + ROWS + 40, cols]
            for a in range(2, 6):
                j = 8 * a + b - 17
                if 0 <= j < TAPS:
                    cwp[j // crow, j % crow : j % crow + 1, cols] = jnp.sum(
                        grad * moved[8 * a : 8 * a + ROWS], axis=0, keepdims=True
                    )
        cwp[Y - 1, crow - 1 : crow, cols] = jnp.zeros((1, 128), F32)
    y_start(YC1)

    for d in range(1, Y):
        head_copy(d, lax.rem(head + Y - d, Y)).wait_recv()
    grad_out = jnp.zeros((ROWS, WIDTH), F32)
    for h in range(Y):
        grad_out = grad_out + nn(xf[h], w[h * WIDTH : (h + 1) * WIDTH, :])
    do_s[...] = grad_out.astype(BF16)
    x_copy(XDO).start()
    dog[0, pl.ds(xh, 1)] = do_s[:, own_cols][None]

    y_recv(YQ)
    first_row = jnp.where(iota((16, BLOCK), 0) == 0, 1.0, 0.0).astype(BF16)
    zero_rows = jnp.zeros((112, BLOCK), BF16)
    for c in range(Y):
        cols = slice(c * BLOCK, (c + 1) * BLOCK)
        scaled = jnp.transpose(qg[c].reshape(BLOCK, PAIR).astype(F32) * (LOG2E * HEAD_DIM**-0.5))
        high = scaled.astype(BF16)
        low = (scaled - high.astype(F32)).astype(BF16)
        for h in range(2):
            rows = slice(h * HEAD_DIM, (h + 1) * HEAD_DIM)
            qta[h, :, cols] = jnp.concatenate([high[rows], low[rows], first_row, zero_rows], axis=0)
    mrun[...] = jnp.full(mrun.shape, NEG, F32)
    ot[...] = jnp.zeros(ot.shape, F32)
    ones_rows = jnp.ones((16, BLOCK), BF16)
    lane = iota((BLOCK, PAIR), 1)

    x_copy(XDO).wait_recv()
    y_start(YDO)

    def forward_step(s, carry):
        i = lax.div(s, 2)
        odd = lax.rem(s, 2)
        slot = lax.rem(odd * (i + 1) + (1 - odd) * (Z - i), Z)

        @pl.when(s > 0)
        def _():
            remote(kv.at[slot], kv.at[slot], kvs.at[slot], kvr.at[slot], z_peer(1)).wait_recv()

        @pl.when((odd == 1) & (s < Z - 1))
        def _():
            remote(kv.at[slot], kv.at[slot + 1], kvs.at[slot + 1], kvr.at[slot + 1], z_peer(1)).start()

        @pl.when((odd == 0) & (s > 0) & (s < Z - 2))
        def _():
            remote(kv.at[slot], kv.at[slot - 1], kvs.at[slot - 1], kvr.at[slot - 1], z_peer(Z - 1)).start()

        keys = kv[slot, 0].reshape(BLOCK, PAIR).astype(F32)
        values = kv[slot, 1].reshape(BLOCK, PAIR).astype(F32)
        kt[slot] = jnp.transpose(keys).astype(BF16)
        values_t = jnp.transpose(values).astype(BF16)
        keys_moved = pltpu.roll(keys, HEAD_DIM, 1)
        values_moved = pltpu.roll(values, HEAD_DIM, 1)
        origin = lax.rem(z + Z - slot, Z)
        row = iota((BLOCK, PAIR), 0)
        position = (y * 2 * Z + origin) * ROWS + lax.div(row, ROWS) * (Z * ROWS) + lax.rem(row, ROWS)
        bias = jnp.where((lane == 0) & (position >= valid), NEG, 0.0).astype(BF16)
        for h in range(2):
            first, second = (keys, keys_moved) if h == 0 else (keys_moved, keys)
            ka[h] = jnp.concatenate([jnp.where(lane < HEAD_DIM, first, second).astype(BF16), bias], axis=1)
            mine = values if h == 0 else values_moved
            extra = jnp.where(lane < HEAD_DIM + 2, 1.0, 0.0)
            va[slot, h] = jnp.where(lane < HEAD_DIM, mine, extra).astype(BF16)
            vta[h] = jnp.concatenate([values_t[h * HEAD_DIM : (h + 1) * HEAD_DIM], ones_rows], axis=0)
        for h in range(2):
            for c in range(Y):
                cols = slice(c * BLOCK, (c + 1) * BLOCK)
                scores = nn(ka[h], qta[h, :, cols])
                old = mrun[h, :, cols]
                new = jnp.maximum(old, jnp.max(scores, axis=0, keepdims=True))
                p16 = jnp.exp2(scores - new).astype(BF16)
                probs[slot, h, :, cols] = p16
                ot[h, :, cols] = ot[h, :, cols] * jnp.exp2(old - new) + nn(vta[h], p16)
                mrun[h, :, cols] = new
                mk[slot, h, :, cols] = new
        return carry

    lax.fori_loop(0, Z, forward_step, 0)

    y_recv(YDO)
    for c in range(Y):
        cols = slice(c * BLOCK, (c + 1) * BLOCK)
        dot_[:, cols] = jnp.transpose(dog[c].reshape(BLOCK, PAIR).astype(F32))
        for h in range(2):
            st[0, c, 3 * h : 3 * h + 1, :] = mrun[h, :, cols]
            st[0, c, 3 * h + 1 : 3 * h + 2, :] = ot[h, HEAD_DIM : HEAD_DIM + 1, cols]
            st[0, c, 3 * h + 2 : 3 * h + 3, :] = jnp.sum(
                ot[h, 0:HEAD_DIM, cols] * dot_[h * HEAD_DIM : (h + 1) * HEAD_DIM, cols], axis=0, keepdims=True
            )
        st[0, c, 6:8, :] = jnp.zeros((2, BLOCK), F32)
    y_start(YST)

    y_recv(YC1)
    total = cwp[y]
    for d in range(1, Y):
        total = total + cwr[d]
    c1[...] = total
    x_copy(XCW).start()
    dqt[...] = jnp.zeros(dqt.shape, F32)

    y_recv(YST)
    for c in range(Y):
        cols = slice(c * BLOCK, (c + 1) * BLOCK)
        parts = []
        for h in range(2):
            rows = [st[e, (c - e) % Y] for e in range(Y)]
            maxima = [r[3 * h : 3 * h + 1] for r in rows]
            top = functools.reduce(jnp.maximum, maxima)
            shrink = [jnp.exp2(m - top) for m in maxima]
            total = sum(r[3 * h + 1 : 3 * h + 2] * f for r, f in zip(rows, shrink))
            delta = sum(r[3 * h + 2 : 3 * h + 3] * f for r, f in zip(rows, shrink))
            inverse = 1.0 / total
            mst[h, :, cols] = top
            lin[h, :, cols] = inverse
            dlt[h, :, cols] = delta * inverse
            parts.append(ot[h, 0:HEAD_DIM, cols] * (shrink[0] * inverse))
        os[c] = jnp.transpose(jnp.concatenate(parts, axis=0)).astype(BF16)
    y_start(YO)

    delta_row = iota((16, BLOCK), 0)
    gbuf[...] = jnp.zeros(gbuf.shape, BF16)

    def backward_step(s, carry):
        i = lax.div(s, 2)
        odd = lax.rem(s, 2)
        slot = odd * (Z // 2 - 1 - i) + (1 - odd) * (Z // 2 + i)
        dk, dv = [], []
        for h in range(2):
            rows = slice(h * HEAD_DIM, (h + 1) * HEAD_DIM)
            for c in range(Y):
                cols = slice(c * BLOCK, (c + 1) * BLOCK)
                factor = jnp.exp2(mk[slot, h, :, cols] - mst[h, :, cols]) * lin[h, :, cols]
                shift = -dlt[h, :, cols] * factor
                high = shift.astype(BF16).astype(F32)
                gbuf[h, 0:HEAD_DIM, cols] = (dot_[rows, cols] * factor).astype(BF16)
                gbuf[h, HEAD_DIM : HEAD_DIM + 16, cols] = jnp.where(
                    delta_row == 0, high, jnp.where(delta_row == 1, shift - high, 0.0)
                ).astype(BF16)
                slopes = nn(va[slot, h], gbuf[h, :, cols])
                ds = (probs[slot, h, :, cols].astype(F32) * slopes).astype(BF16)
                dsb[h, :, cols] = ds
                dqt[rows, cols] += nn(kt[slot, rows, :], ds)
            dv.append(nt(probs[slot, h], gbuf[h, 0:HEAD_DIM, :]))
            dk.append(nn(dsb[h], qg[...].reshape(Q, PAIR)))
        acc[0] = jnp.where(lane < HEAD_DIM, dk[0], dk[1]) * HEAD_DIM**-0.5
        acc[1] = jnp.concatenate(dv, axis=1)

        @pl.when(s >= 2)
        def _():
            rs_copy(s - 2, z_peer(1)).wait_recv()
            acc[...] += rsr[s - 2].astype(F32)

        @pl.when(s < Z - 1)
        def _():
            rss[s] = acc[...].astype(BF16)
            rs_copy(s, at(y, xh, lax.rem(z + 1 + odd * (Z - 2), Z))).start()

        @pl.when(s == 0)
        def _():
            x_copy(XCW).wait_recv()
            cz[pl.ds(z, 1)] = (c1[...] + cx[...])[None]
            for d in range(1, Z):
                cz_copy(d).start()
            y_recv(YO)
            out = os[0].astype(F32)
            for d in range(1, Y):
                out = out + orr[d].astype(F32)
            of[...] = out.astype(BF16).reshape(2, ROWS, PAIR)
            x_copy(XO).start()

        @pl.when(s == 1)
        def _():
            x_copy(XO).wait_recv()
            mine, theirs = of[pl.ds(xh, 1)].reshape(ROWS, PAIR), ox[...]
            low = jnp.where(xh == 0, mine.astype(F32), theirs.astype(F32))
            high = jnp.where(xh == 0, theirs.astype(F32), mine.astype(F32))
            attn = jnp.concatenate([low, high], axis=1).astype(BF16)
            for h in range(Y):
                gs[h] = tn(xf[h], attn).astype(BF16).reshape(2, ROWS, WIDTH)
            y_start(YG)

        @pl.when(s == Z - 4)
        def _():
            y_recv(YG)
            sums = gs[pl.ds(y, 1)].reshape(2, ROWS, WIDTH).astype(F32)
            for d in range(1, Y):
                sums = sums + gr[d].astype(F32)
            gy[...] = sums.astype(BF16)
            x_copy(XG).start()
            for d in range(1, Z):
                remote(
                    cz.at[z], cz.at[lax.rem(z + Z - d, Z)], czs.at[d], czr.at[d], z_peer(d)
                ).wait_recv()
            total = cz[0]
            for d in range(1, Z):
                total = total + cz[d]
            cfin[pl.ds(y, 1)] = total[None]
            y_start(YC2)

        @pl.when(s == Z - 3)
        def _():
            x_copy(XG).wait_recv()
            sums = gy[pl.ds(xh, 1)].reshape(ROWS, WIDTH).astype(F32) + gx[...].astype(F32)
            sums = sums.reshape(Z, ROWS // Z, WIDTH)
            gt[...] = sums
            gz[...] = sums.astype(BF16)
            for d in range(1, Z):
                gz_copy(d).start()

        @pl.when(s == Z - 1)
        def _():
            for d in range(1, Z):
                gz_copy(d).wait_recv()
            sums = gt[pl.ds(z, 1)].reshape(ROWS // Z, WIDTH)
            for d in range(1, Z):
                sums = sums + gzr[d].astype(F32)
            g_o[...] = sums

        return carry

    lax.fori_loop(0, Z, backward_step, 0)

    for c in list(range(1, Y)) + [0]:
        dqs[c] = jnp.transpose(dqt[:, c * BLOCK : (c + 1) * BLOCK] * HEAD_DIM**-0.5).astype(BF16)
        if c:
            y_copy(YDQ, Y - c).start()
    rs_copy(Z - 2, z_peer(1)).wait_recv()
    fk[...] = (acc[...] + rsr[Z - 2].astype(F32)).astype(BF16).reshape(2, 2, ROWS, PAIR)
    x_copy(XDK).start()
    x_copy(XDV).start()
    k_o[:, own_cols] = fk[0, pl.ds(xh, 1)].reshape(ROWS, PAIR)
    v_o[:, own_cols] = fk[1, pl.ds(xh, 1)].reshape(ROWS, PAIR)

    for d in range(1, Y):
        slot = lax.rem(y + Y - d, Y)
        remote(cfin.at[slot], cfin.at[slot], ys.at[YC2, d], yr.at[YC2, d], y_peer(d)).wait_recv()
    for h in range(Y):
        count = min(crow, TAPS - h * crow)
        c_o[h * crow : h * crow + count, :] = cfin[h, 0:count, :]

    y_recv(YDQ)
    total = dqs[0].astype(F32)
    for d in range(1, Y):
        total = total + dqr[d].astype(F32)
    fq[...] = total.astype(BF16).reshape(2, ROWS, PAIR)
    x_copy(XDQ).start()
    q_o[:, own_cols] = fq[pl.ds(xh, 1)].reshape(ROWS, PAIR)

    for i in (XDK, XDV, XDQ):
        x_copy(i).wait_recv()
    for i in range(4):
        halo(i).wait_send()
    for i in range(10):
        x_copy(i).wait_send()
    for i in range(8):
        for d in range(1, Y):
            y_copy(i, d).wait_send()
    for d in range(1, Y):
        head_copy(d, head).wait_send()
    for slot in range(1, Z):
        kv_copy(slot).wait_send()
    for s in range(Z - 1):
        rs_copy(s, z_peer(1)).wait_send()
    for d in range(1, Z):
        gz_copy(d).wait_send()
        cz_copy(d).wait_send()


def on_device(Y, Z, query_all, key_all, value_all, cotangent, conv_input, rec_lengths, out_proj, conv_weight):
    Q = Y * BLOCK
    vm, dma = pltpu.VMEM, pltpu.SemaphoreType.DMA
    vmem = pl.BlockSpec(memory_space=pltpu.VMEM)
    crow = 32 // Y
    block = (ROWS, WIDTH)
    scratch = [
        vm((Z, 2, 2, ROWS, PAIR), BF16),
        vm((Y, 2, ROWS, PAIR), BF16),
        vm((Y, 2, ROWS, PAIR), BF16),
        vm((Z, PAIR, BLOCK), BF16),
        vm((Z, 2, BLOCK, PAIR), BF16),
        vm((2, BLOCK, 2 * PAIR), BF16),
        vm((2, HEAD_DIM + 16, BLOCK), BF16),
        vm((2, 2 * PAIR, Q), BF16),
        vm((Z, 2, BLOCK, Q), BF16),
        vm((Z, 2, 1, Q), F32),
        vm((2, 1, Q), F32),
        vm((2, HEAD_DIM + 16, Q), F32),
        vm((PAIR, Q), F32),
        vm((PAIR, Q), F32),
        vm((2, 1, Q), F32),
        vm((2, 1, Q), F32),
        vm((2, 1, Q), F32),
        vm((2, PAIR, Q), BF16),
        vm((2, BLOCK, Q), BF16),
        vm((2, 32, WIDTH), BF16),
        vm((2, 16, WIDTH), BF16),
        vm((ROWS + 64, WIDTH), F32),
        vm((ROWS + 32, WIDTH), F32),
        vm((Y, ROWS, WIDTH), BF16),
        vm(block, BF16),
        vm((Y, Y, 8, BLOCK), F32),
        vm((Y, BLOCK, PAIR), BF16),
        vm((Y, BLOCK, PAIR), BF16),
        vm((2, ROWS, PAIR), BF16),
        vm((ROWS, PAIR), BF16),
        vm((Y, 2, ROWS, WIDTH), BF16),
        vm((Y, 2, ROWS, WIDTH), BF16),
        vm((2, ROWS, WIDTH), BF16),
        vm(block, BF16),
        vm((Z, ROWS // Z, WIDTH), F32),
        vm((Z, ROWS // Z, WIDTH), BF16),
        vm((Z, ROWS // Z, WIDTH), BF16),
        vm((2, BLOCK, PAIR), F32),
        vm((Z, 2, BLOCK, PAIR), BF16),
        vm((Z, 2, BLOCK, PAIR), BF16),
        vm((2, 2, ROWS, PAIR), BF16),
        vm((Y, BLOCK, PAIR), BF16),
        vm((Y, BLOCK, PAIR), BF16),
        vm((2, ROWS, PAIR), BF16),
        vm((Y, crow, WIDTH), F32),
        vm((Y, crow, WIDTH), F32),
        vm((crow, WIDTH), F32),
        vm((crow, WIDTH), F32),
        vm((Z, crow, WIDTH), F32),
        vm((Y, crow, WIDTH), F32),
        dma((4,)), dma((4,)),
        dma((Y,)), dma((Y,)),
        dma((10,)), dma((10,)),
        dma((8, Y)), dma((8, Y)),
        dma((Z,)), dma((Z,)),
        dma((Z,)), dma((Z,)),
        dma((Z,)), dma((Z,)),
        dma((Z,)), dma((Z,)),
    ]
    return pl.pallas_call(
        functools.partial(fused_kernel, Y, Z),
        out_shape=(
            jax.ShapeDtypeStruct(block, BF16),
            jax.ShapeDtypeStruct(block, BF16),
            jax.ShapeDtypeStruct(block, BF16),
            jax.ShapeDtypeStruct(block, BF16),
            jax.ShapeDtypeStruct((ROWS // Z, WIDTH), F32),
            jax.ShapeDtypeStruct((TAPS, WIDTH), F32),
        ),
        in_specs=[pl.BlockSpec(memory_space=pltpu.SMEM)] + [vmem] * 7,
        out_specs=(vmem,) * 6,
        scratch_shapes=scratch,
        compiler_params=pltpu.CompilerParams(
            collective_id=0, has_side_effects=True, vmem_limit_bytes=56 * 1024 * 1024
        ),
        name="conv_attention_backward",
    )(rec_lengths, query_all, key_all, value_all, cotangent, conv_input, out_proj, conv_weight)


def solution(mesh):
    sizes = dict(mesh.shape)
    Y = sizes["head"]
    Z = sizes["ctx"] // (2 * Y)
    both = P("ctx", "head")
    return jax.shard_map(
        functools.partial(on_device, Y, Z),
        mesh=mesh,
        in_specs=(both, both, both, both, both, P(), P(None, "head"), P(None, "head")),
        out_specs=(both, both, both, both, both, P(None, "head")),
        check_vma=False,
    )
```

```python
import functools

import jax
import jax.numpy as jnp
from jax import lax
from jax.experimental import pallas as pl
from jax.experimental.pallas import tpu as pltpu
from jax.sharding import PartitionSpec as P

F32, BF16 = jnp.float32, jnp.bfloat16
HEAD_DIM = 64
ROWS = 128
WIDTH = 256
PAIR = 128
BLOCK = 256
TAPS = 31
NEG = -1e30
LOG2E = 1.4426950408889634
MESH = pl.DeviceIdType.MESH


def nt(a, b):
    return lax.dot_general(a, b, (((1,), (1,)), ((), ())), preferred_element_type=F32)


def tn(a, b):
    return lax.dot_general(a, b, (((0,), (0,)), ((), ())), preferred_element_type=F32)


def nn(a, b):
    return jnp.dot(a, b, preferred_element_type=F32)


def iota(shape, dim):
    return lax.broadcasted_iota(jnp.int32, shape, dim)


def fused_kernel(
    Y, Z,
    rec, q_in, k_in, v_in, ct_in, ci_in, w_in, taps,
    q_out, k_out, v_out, x_out, g_out, c_out,
    q, k, v, ct, ci, w, q_o, k_o, v_o, x_o, g_o, c_o, load_s, store_s,
    kv, qg, dog, kt, va, ka, vta, qta, probs, mk, mrun, ot, dot_, dqt, mst, lin, dlt, wts, gbuf, dsb,
    hci, hct, ext, gex, xf, xfp, do_s,
    st, os, orr, attn, gs, gr, gt, gz, gzr,
    part, rss, rsr, fin, dqs, dqr,
    cwp, cwr, c1, cx, cz, cfin,
    halo_s, halo_r, head_s, head_r, xs, xr, ys, yr, yxs, yxr, kvs, kvr, rs_s, rs_r, fin_s, fin_r, gzs, gzrs, czs, czr,
):
    Q = Y * BLOCK
    N = 2 * Y * Z
    HALF = Z // 2
    ctx, head = lax.axis_index("ctx"), lax.axis_index("head")
    y = lax.div(ctx, 2 * Z)
    xh = lax.rem(lax.div(ctx, Z), 2)
    z = lax.rem(ctx, Z)
    other = 1 - xh
    sides = (xh, other)

    def at(yy, xx, zz):
        return ((yy * 2 + xx) * Z + zz, head)

    def plus_y(d):
        return lax.rem(y + d, Y)

    def plus_z(d):
        return lax.rem(z + d, Z)

    def y_peer(d):
        return at(plus_y(d), xh, z)

    def z_peer(d):
        return at(y, xh, plus_z(d))

    def head_peer(d):
        return (ctx, lax.rem(head + d, Y))

    partner = at(y, other, z)
    following = (lax.rem(ctx + 1, N), head)
    preceding = (lax.rem(ctx + N - 1, N), head)

    def remote(src, dst, send, recv, device):
        return pltpu.make_async_remote_copy(
            src_ref=src, dst_ref=dst, send_sem=send, recv_sem=recv, device_id=device, device_id_type=MESH
        )

    own_cols = pl.ds(pl.multiple_of(xh * PAIR, PAIR), PAIR)
    other_cols = pl.ds(pl.multiple_of(other * PAIR, PAIR), PAIR)
    side_cols = (own_cols, other_cols)

    def halo(i):
        src, dst, dev = (
            (ci.at[pl.ds(ROWS - 32, 32)], hci.at[0], following),
            (ci.at[pl.ds(0, 32)], hci.at[1], preceding),
            (ct.at[pl.ds(ROWS - 16, 16)], hct.at[0], following),
            (ct.at[pl.ds(0, 16)], hct.at[1], preceding),
        )[i]
        return remote(src, dst, halo_s.at[i], halo_r.at[i], dev)

    XK, XV, XQ, XF, XCW = range(5)

    def x_copy(i):
        src, dst = (
            lambda: (k.at[:, other_cols], kv.at[0, 0, xh]),
            lambda: (v.at[:, other_cols], kv.at[0, 1, xh]),
            lambda: (q.at[:, other_cols], qg.at[0, xh]),
            lambda: (xf, xfp),
            lambda: (c1, cx),
        )[i]()
        return remote(src, dst, xs.at[i], xr.at[i], partner)

    def x_recv(i):
        if i < XF:
            dst = (kv.at[0, 0, other], kv.at[0, 1, other], qg.at[0, other])[i]
            remote(dst, dst, xs.at[i], xr.at[i], partner).wait_recv()
        else:
            x_copy(i).wait_recv()

    YQ, YST, YO, YG, YC1, YC2 = range(6)

    def y_copy(i, d):
        src, dst = (
            lambda: (qg.at[0], qg.at[d]),
            lambda: (st.at[0], st.at[d]),
            lambda: (os.at[Y - d], orr.at[d]),
            lambda: (gs.at[plus_y(d)], gr.at[d]),
            lambda: (cwp.at[plus_y(d)], cwr.at[d]),
            lambda: (cfin.at[y], cfin.at[y]),
        )[i]()
        return remote(src, dst, ys.at[i, d], yr.at[i, d], y_peer(d))

    def y_start(i):
        for d in range(1, Y):
            y_copy(i, d).start()

    def y_recv(i):
        for d in range(1, Y):
            y_copy(i, d).wait_recv()

    spread = [(d, e) for d in range(Y) for e in range(2) if d or e]
    SDO, SDQ = range(2)

    def spread_copy(i, d, e):
        src, dst = (
            lambda: (do_s.at[:, side_cols[e]], dog.at[d, xh]),
            lambda: (dqs.at[(Y - d) % Y, sides[e]], dqr.at[d, e]),
        )[i]()
        return remote(src, dst, yxs.at[i, d, e], yxr.at[i, d, e], at(plus_y(d), sides[e], z))

    def spread_recv(i):
        for d, e in spread:
            dst = dog.at[d, sides[e]] if i == SDO else dqr.at[d, e]
            remote(dst, dst, yxs.at[i, d, e], yxr.at[i, d, e], partner).wait_recv()

    def ring(src, dst, j, device):
        piece = (j % 2, sides[j // 2])
        return remote(kv.at[(src, *piece)], kv.at[(dst, *piece)], kvs.at[dst, j], kvr.at[dst, j], device)

    def ring_start(j):
        ring(0, 1, j, z_peer(1)).start()
        ring(0, Z - 1, j, z_peer(Z - 1)).start()

    def ring_event(level, j):
        ring(level, level, j, partner).wait_recv()

        @pl.when(level < HALF)
        def _():
            ring(level, level + 1, j, z_peer(1)).start()

        @pl.when(level < HALF)
        def _():
            ring(Z - level, Z - level, j, partner).wait_recv()

        @pl.when(level < HALF - 1)
        def _():
            ring(Z - level, Z - level - 1, j, z_peer(Z - 1)).start()

    shares = [(d, e) for d in range(Z) for e in range(2) if d or e]

    def gz_copy(d, e):
        return remote(
            gz.at[sides[e], plus_z(d)], gzr.at[e, d], gzs.at[e, d], gzrs.at[e, d], at(y, sides[e], plus_z(d))
        )

    def cz_copy(d):
        return remote(cz.at[z], cz.at[z], czs.at[d], czr.at[d], z_peer(d))

    loads = ((k_in, k), (v_in, v), (q_in, q), (ci_in, ci), (ct_in, ct), (None, None), (w_in, w))
    stores = ((x_o, x_out), (c_o, c_out), (g_o, g_out), (k_o, k_out), (v_o, v_out), (q_o, q_out))

    def load(i):
        return pltpu.make_async_copy(*loads[i], load_s.at[i])

    def store(i):
        return pltpu.make_async_copy(*stores[i], store_s.at[i])

    for i in (0, 1, 2, 3, 4, 6):
        load(i).start()
    peers = [partner, following, preceding, z_peer(1), z_peer(Z - 1)]
    peers += [y_peer(d) for d in range(1, Y)] + [head_peer(d) for d in range(1, Y)]
    barrier = pltpu.get_barrier_semaphore()
    for peer in peers:
        pl.semaphore_signal(barrier, inc=1, device_id=peer, device_id_type=MESH)
    for i in range(5):
        load(i).wait()
    kv[0, 0, pl.ds(xh, 1)] = k[:, own_cols][None]
    kv[0, 1, pl.ds(xh, 1)] = v[:, own_cols][None]
    qg[0, pl.ds(xh, 1)] = q[:, own_cols][None]
    pl.semaphore_wait(barrier, len(peers))

    for i in range(4):
        halo(i).start()
    for i in (XK, XV, XQ):
        x_copy(i).start()
    for j in range(2):
        ring_start(j)
    valid = rec[0] + rec[1] + rec[2]

    for i in (0, 1):
        halo(i).wait_recv()
    pos = ctx * ROWS - 32 + iota((ROWS + 64, WIDTH), 0)
    ext[...] = jnp.where(
        (pos >= 0) & (pos < valid), jnp.concatenate([hci[0], ci[...], hci[1]], axis=0).astype(F32), 0.0
    )
    for i in (2, 3):
        halo(i).wait_recv()
    weights = taps[...].astype(F32)
    for c in range(2):
        cols = slice(c * 128, c * 128 + 128)
        conv = jnp.zeros((ROWS + 32, 128), F32)
        for b in range(8):
            moved = ext[b : b + ROWS + 56, cols]
            for a in range(4):
                j = 8 * a + b - 1
                if 0 <= j < TAPS:
                    conv = conv + weights[j : j + 1, cols] * moved[8 * a : 8 * a + ROWS + 32]
        sig = jax.nn.sigmoid(conv)
        up = jnp.concatenate([hct[0, :, cols], ct[:, cols], hct[1, :, cols]], axis=0).astype(F32)
        slope = (up * sig * (1.0 + conv * (1.0 - sig))).astype(BF16).astype(F32)
        gpos = ctx * ROWS - 16 + iota((ROWS + 32, 128), 0)
        gex[:, cols] = jnp.where((gpos >= 0) & (gpos < N * ROWS), slope, 0.0)

    for i, j in ((XK, 2), (XV, 3)):
        x_recv(i)
        ring_start(j)
    x_recv(XQ)
    y_start(YQ)

    for c in range(2):
        cols = slice(c * 128, c * 128 + 128)
        back = jnp.zeros((ROWS, 128), F32)
        for b in range(8):
            moved = gex[b : b + ROWS + 24, cols]
            for a in range(4):
                j = TAPS - 8 * a - b
                if 0 <= j < TAPS:
                    back = back + weights[j : j + 1, cols] * moved[8 * a : 8 * a + ROWS]
        frame = ctx * ROWS + iota((ROWS, 128), 0)
        x16 = (ct[:, cols].astype(F32) + jnp.where(frame < valid, back, 0.0)).astype(BF16)
        x_o[:, cols] = x16
        xf[pl.ds(head, 1), :, cols] = x16[None]

    def head_copy(d, slot):
        return remote(xf.at[slot], xf.at[slot], head_s.at[d], head_r.at[d], head_peer(d))

    for d in range(1, Y):
        head_copy(d, head).start()
    store(0).start()
    for j in range(4):
        ring_event(1, j)

    crow = 32 // Y
    for c in range(2):
        cols = slice(c * 128, c * 128 + 128)
        grad = gex[16 : 16 + ROWS, cols]
        for b in range(8):
            moved = ext[b : b + ROWS + 40, cols]
            for a in range(2, 6):
                j = 8 * a + b - 17
                if 0 <= j < TAPS:
                    cwp[j // crow, j % crow : j % crow + 1, cols] = jnp.sum(
                        grad * moved[8 * a : 8 * a + ROWS], axis=0, keepdims=True
                    )
        cwp[Y - 1, crow - 1 : crow, cols] = jnp.zeros((1, 128), F32)
    y_start(YC1)

    y_recv(YQ)
    first_row = jnp.where(iota((16, BLOCK), 0) == 0, 1.0, 0.0).astype(BF16)
    zero_rows = jnp.zeros((112, BLOCK), BF16)
    for c in range(Y):
        cols = slice(c * BLOCK, (c + 1) * BLOCK)
        scaled = jnp.transpose(qg[c].reshape(BLOCK, PAIR).astype(F32) * (LOG2E * HEAD_DIM**-0.5))
        high = scaled.astype(BF16)
        low = (scaled - high.astype(F32)).astype(BF16)
        for h in range(2):
            rows = slice(h * HEAD_DIM, (h + 1) * HEAD_DIM)
            qta[h, :, cols] = jnp.concatenate([high[rows], low[rows], first_row, zero_rows], axis=0)

    ones_rows = jnp.ones((16, BLOCK), BF16)
    lane = iota((BLOCK, PAIR), 1)

    def prepare(slot, place):
        keys = kv[slot, 0].reshape(BLOCK, PAIR).astype(F32)
        values = kv[slot, 1].reshape(BLOCK, PAIR).astype(F32)
        kt[slot] = jnp.transpose(keys).astype(BF16)
        values_t = jnp.transpose(values).astype(BF16)
        keys_moved = pltpu.roll(keys, HEAD_DIM, 1)
        values_moved = pltpu.roll(values, HEAD_DIM, 1)
        origin = lax.rem(z + Z - slot, Z)
        row = iota((BLOCK, PAIR), 0)
        position = (y * 2 * Z + origin) * ROWS + lax.div(row, ROWS) * (Z * ROWS) + lax.rem(row, ROWS)
        bias = jnp.where((lane == 0) & (position >= valid), NEG, 0.0).astype(BF16)
        for h in range(2):
            first, second = (keys, keys_moved) if h == 0 else (keys_moved, keys)
            ka[place, h] = jnp.concatenate(
                [jnp.where(lane < HEAD_DIM, first, second).astype(BF16), bias], axis=1
            )
            mine = values if h == 0 else values_moved
            extra = jnp.where(lane < HEAD_DIM + 2, 1.0, 0.0)
            va[slot, h] = jnp.where(lane < HEAD_DIM, mine, extra).astype(BF16)
            vta[place, h] = jnp.concatenate([values_t[h * HEAD_DIM : (h + 1) * HEAD_DIM], ones_rows], axis=0)

    def forward_unit(slot, place, h):
        scores = nn(ka[place, h], qta[h])
        old = mrun[h]
        new = jnp.maximum(old, jnp.max(scores, axis=0, keepdims=True))
        p16 = jnp.exp2(scores - new).astype(BF16)
        probs[slot, h] = p16
        ot[h] = ot[h] * jnp.exp2(old - new) + nn(vta[place, h], p16)
        mrun[h] = new
        mk[slot, h] = new

    mrun[...] = jnp.full(mrun.shape, 2 * NEG, F32)
    ot[...] = jnp.zeros(ot.shape, F32)
    prepare(0, 0)
    for h in range(2):
        forward_unit(0, 0, h)

    for d in range(1, Y):
        head_copy(d, lax.rem(head + Y - d, Y)).wait_recv()
    load(6).wait()
    grad_out = jnp.zeros((ROWS, WIDTH), F32)
    for h in range(Y):
        grad_out = grad_out + nn(xf[h], w[h * WIDTH : (h + 1) * WIDTH, :])
    do_s[...] = grad_out.astype(BF16)
    for d, e in spread:
        spread_copy(SDO, d, e).start()
    dog[0, pl.ds(xh, 1)] = do_s[:, own_cols][None]
    x_copy(XF).start()

    def forward_step(d, carry):
        prepare(d, 0)

        @pl.when(d < HALF)
        def _():
            prepare(Z - d, 1)

        for j in range(4):

            @pl.when(d < HALF)
            def _():
                ring_event(d + 1, j)

            if j < 2:
                forward_unit(d, 0, j)
            else:

                @pl.when(d < HALF)
                def _():
                    forward_unit(Z - d, 1, j - 2)

        return carry

    lax.fori_loop(1, HALF + 1, forward_step, 0)

    spread_recv(SDO)
    for c in range(Y):
        cols = slice(c * BLOCK, (c + 1) * BLOCK)
        dot_[:, cols] = jnp.transpose(dog[c].reshape(BLOCK, PAIR).astype(F32))
        parts = []
        for h in range(2):
            out = ot[h, 0:HEAD_DIM, cols]
            total = ot[h, HEAD_DIM : HEAD_DIM + 1, cols]
            st[0, c, 3 * h : 3 * h + 1, :] = mrun[h, :, cols]
            st[0, c, 3 * h + 1 : 3 * h + 2, :] = total
            st[0, c, 3 * h + 2 : 3 * h + 3, :] = jnp.sum(
                out * dot_[h * HEAD_DIM : (h + 1) * HEAD_DIM, cols], axis=0, keepdims=True
            )
            parts.append(out / total)
        st[0, c, 6:8, :] = jnp.zeros((2, BLOCK), F32)
        os[c] = jnp.concatenate(parts, axis=0).astype(BF16)
    y_start(YST)
    y_start(YO)

    y_recv(YC1)
    total = cwp[y]
    for d in range(1, Y):
        total = total + cwr[d]
    c1[...] = total
    x_copy(XCW).start()
    dqt[...] = jnp.zeros(dqt.shape, F32)
    gbuf[...] = jnp.zeros(gbuf.shape, BF16)

    y_recv(YST)
    for c in range(Y):
        cols = slice(c * BLOCK, (c + 1) * BLOCK)
        rows = [st[e, (c - e) % Y] for e in range(Y)]
        for h in range(2):
            maxima = [r[3 * h : 3 * h + 1] for r in rows]
            top = functools.reduce(jnp.maximum, maxima)
            shrink = [jnp.exp2(m - top) for m in maxima]
            totals = [r[3 * h + 1 : 3 * h + 2] * f for r, f in zip(rows, shrink)]
            delta = sum(r[3 * h + 2 : 3 * h + 3] * f for r, f in zip(rows, shrink))
            inverse = 1.0 / sum(totals)
            mst[h, :, cols] = top
            lin[h, :, cols] = inverse
            dlt[h, :, cols] = delta * inverse
            if c == 0:
                for e in range(Y):
                    wts[e, h] = totals[e] * inverse

    delta_row = iota((16, Q), 0)

    def backward_unit(slot, place, parity, h):
        rows = slice(h * HEAD_DIM, (h + 1) * HEAD_DIM)
        factor = jnp.exp2(mk[slot, h] - mst[h]) * lin[h]
        shift = -dlt[h] * factor
        high = shift.astype(BF16).astype(F32)
        gbuf[h, 0:HEAD_DIM] = (dot_[rows] * factor).astype(BF16)
        gbuf[h, HEAD_DIM : HEAD_DIM + 16] = jnp.where(
            delta_row == 0, high, jnp.where(delta_row == 1, shift - high, 0.0)
        ).astype(BF16)
        slopes = nn(va[slot, h], gbuf[h])
        ds = (probs[slot, h].astype(F32) * slopes).astype(BF16)
        dsb[h] = ds
        dqt[rows] += nn(kt[slot, rows, :], ds)
        dk = nn(dsb[h], qg[...].reshape(Q, PAIR))
        part[place, parity, 0, :, rows] = dk[:, rows] * HEAD_DIM**-0.5
        part[place, parity, 1, :, rows] = nt(probs[slot, h], gbuf[h, 0:HEAD_DIM, :])

    def rs_copy(place, level, t, half, device):
        return remote(
            rss.at[place, level, t, half], rsr.at[place, level, t, half],
            rs_s.at[place, level, t, half], rs_r.at[place, level, t, half], device,
        )

    def fin_copy(kind, e, t, src):
        zz = (plus_z(1), plus_z(Z - 1), z)[kind]
        return remote(
            src, fin.at[kind, e, t], fin_s.at[kind, e, t], fin_r.at[kind, e, t], at(y, sides[e], zz)
        )

    def back_event(place, level, parity, j):
        t, half = j % 2, j // 2
        last = HALF - 1 - place
        rows = slice(half * ROWS, half * ROWS + ROWS)

        @pl.when(level > 0)
        def _():
            @pl.when(level <= last)
            def _():
                rs_copy(place, level - 1, t, half, partner).wait_recv()
                part[place, parity, t, rows] += rsr[place, level - 1, t, half].astype(F32)

        rss[place, level, t, half] = part[place, parity, t, rows].astype(BF16)

        @pl.when(level < last)
        def _():
            rs_copy(place, level, t, half, z_peer(1 if place == 0 else Z - 1)).start()

    def finish_event(place, level, kind):
        for e in range(2):
            for t in range(2):
                if kind < 2 or e == 1:
                    fin_copy(kind, e, t, rss.at[place, level, t, sides[e]]).start()

    for place in range(2):
        for h in range(2):
            backward_unit(HALF if place == 0 else HALF - 1, place, 0, h)
        for j in range(4):
            back_event(place, 0, 0, j)

    def backward_step(i, carry):
        parity = lax.rem(i, 2)
        ahead = 1 - parity

        for j in range(4):

            @pl.when(i > 0)
            def _():
                back_event(0, i, parity, j)
                back_event(1, i, parity, j)

            @pl.when(i < HALF - 1)
            def _():
                place, h = j // 2, j % 2
                backward_unit((HALF + 1 + i) if place == 0 else (HALF - 2 - i), place, ahead, h)

        @pl.when(i == HALF - 2)
        def _():
            finish_event(1, HALF - 2, 1)

        @pl.when(i == HALF - 1)
        def _():
            finish_event(1, HALF - 1, 2)
            finish_event(0, HALF - 1, 0)

        @pl.when(i == 0)
        def _():
            x_recv(XCW)
            cz[pl.ds(z, 1)] = (c1[...] + cx[...])[None]
            for d in range(1, Z):
                cz_copy(d).start()
            y_recv(YO)
            parts = []
            for h in range(2):
                rows = slice(h * HEAD_DIM, (h + 1) * HEAD_DIM)
                parts.append(
                    sum((os if e == 0 else orr)[e, rows, :].astype(F32) * wts[e, h] for e in range(Y))
                )
            attn[...] = jnp.transpose(jnp.concatenate(parts, axis=0)).astype(BF16).reshape(2, ROWS, PAIR)
            x_recv(XF)
            mine = attn[pl.ds(xh, 1)].reshape(ROWS, PAIR)
            theirs = attn[pl.ds(other, 1)].reshape(ROWS, PAIR)
            for h in range(Y):
                gs[h] = (tn(xf[h], mine) + tn(xfp[h], theirs)).astype(BF16)
            y_start(YG)

        @pl.when(i == min(2, HALF - 1))
        def _():
            y_recv(YG)
            sums = gs[pl.ds(y, 1)].reshape(WIDTH, PAIR).astype(F32)
            for d in range(1, Y):
                sums = sums + gr[d].astype(F32)
            sums = sums.reshape(2, Z, ROWS // Z, PAIR)
            gt[...] = sums
            gz[...] = sums.astype(BF16)
            for d, e in shares:
                gz_copy(d, e).start()
            for d in range(1, Z):
                slot = plus_z(Z - d)
                remote(cz.at[slot], cz.at[slot], czs.at[d], czr.at[d], partner).wait_recv()
            total = cz[0]
            for d in range(1, Z):
                total = total + cz[d]
            cfin[pl.ds(y, 1)] = total[None]
            y_start(YC2)

        return carry

    lax.fori_loop(0, HALF, backward_step, 0)

    for c in list(range(1, Y)) + [0]:
        dqs[c] = (
            jnp.transpose(dqt[:, c * BLOCK : (c + 1) * BLOCK] * HEAD_DIM**-0.5)
            .astype(BF16)
            .reshape(2, ROWS, PAIR)
        )
        for e in range(2):
            if c or e:
                spread_copy(SDQ, (Y - c) % Y, e).start()

    for d in range(1, Y):
        slot = plus_y(Y - d)
        remote(cfin.at[slot], cfin.at[slot], ys.at[YC2, d], yr.at[YC2, d], partner).wait_recv()
    for h in range(Y):
        count = min(crow, TAPS - h * crow)
        c_o[h * crow : h * crow + count, :] = cfin[h, 0:count, :]
    store(1).start()

    for d, e in shares:
        gz_copy(d, e).wait_recv()
    for e in range(2):
        sums = gt[pl.ds(xh, 1), pl.ds(z, 1)].reshape(ROWS // Z, PAIR) if e == 0 else gzr[1, 0].astype(F32)
        for d in range(1, Z):
            sums = sums + gzr[e, d].astype(F32)
        g_o[:, side_cols[e]] = sums
    store(2).start()

    for t, out in ((0, k_o), (1, v_o)):
        for e in range(2):
            for kind in range(3):
                if kind < 2 or e == 1:
                    fin_copy(kind, e, t, fin.at[kind, e, t]).wait_recv()
            total = fin[0, e, t].astype(F32) + fin[1, e, t].astype(F32)
            if e == 0:
                start = pl.multiple_of(xh * ROWS, ROWS)
                total = total + part[1, (HALF - 1) % 2, t, pl.ds(start, ROWS), :]
            else:
                total = total + fin[2, 1, t].astype(F32)
            out[:, side_cols[e]] = total.astype(BF16)
        store(3 + t).start()

    spread_recv(SDQ)
    for e in range(2):
        total = dqs[0, pl.ds(xh, 1)].reshape(ROWS, PAIR).astype(F32) if e == 0 else dqr[0, 1].astype(F32)
        for d in range(1, Y):
            total = total + dqr[d, e].astype(F32)
        q_o[:, side_cols[e]] = total.astype(BF16)
    store(5).start()

    for i in range(4):
        halo(i).wait_send()
    for i in range(5):
        x_copy(i).wait_send()
    for i in range(6):
        for d in range(1, Y):
            y_copy(i, d).wait_send()
    for i in range(2):
        for d, e in spread:
            spread_copy(i, d, e).wait_send()
    for d in range(1, Y):
        head_copy(d, head).wait_send()
    for slot in range(1, Z):
        for j in range(4):
            ring(slot, slot, j, partner).wait_send()
    for t in range(2):
        for half in range(2):
            for level in range(HALF - 1):
                rs_copy(0, level, t, half, partner).wait_send()
            for level in range(HALF - 2):
                rs_copy(1, level, t, half, partner).wait_send()
        for e in range(2):
            for kind in range(3):
                if kind < 2 or e == 1:
                    fin_copy(kind, e, t, fin.at[kind, e, t]).wait_send()
    for d, e in shares:
        gz_copy(d, e).wait_send()
    for d in range(1, Z):
        cz_copy(d).wait_send()
    for i in range(6):
        store(i).wait()


def store_kernel(*refs):
    half = len(refs) // 2
    for source, target in zip(refs[:half], refs[half:]):
        target[...] = source[...]


def on_device(Y, Z, query_all, key_all, value_all, cotangent, conv_input, rec_lengths, out_proj, conv_weight):
    Q = Y * BLOCK
    vm, dma = pltpu.VMEM, pltpu.SemaphoreType.DMA
    vmem = pl.BlockSpec(memory_space=pltpu.VMEM)
    crow = 32 // Y
    block = (ROWS, WIDTH)
    anywhere = pl.BlockSpec(memory_space=pl.ANY)
    scratch = [vm(block, BF16) for name in ("q", "k", "v", "ct", "ci")]
    scratch += [vm((Y * WIDTH, WIDTH), BF16)]
    scratch += [vm(block, BF16) for name in ("q_o", "k_o", "v_o", "x_o")]
    scratch += [
        vm((ROWS // Z, WIDTH), F32),
        vm((TAPS, WIDTH), F32),
        dma((7,)),
        dma((6,)),
        vm((Z, 2, 2, ROWS, PAIR), BF16),
        vm((Y, 2, ROWS, PAIR), BF16),
        vm((Y, 2, ROWS, PAIR), BF16),
        vm((Z, PAIR, BLOCK), BF16),
        vm((Z, 2, BLOCK, PAIR), BF16),
        vm((2, 2, BLOCK, 2 * PAIR), BF16),
        vm((2, 2, HEAD_DIM + 16, BLOCK), BF16),
        vm((2, 2 * PAIR, Q), BF16),
        vm((Z, 2, BLOCK, Q), BF16),
        vm((Z, 2, 1, Q), F32),
        vm((2, 1, Q), F32),
        vm((2, HEAD_DIM + 16, Q), F32),
        vm((PAIR, Q), F32),
        vm((PAIR, Q), F32),
        vm((2, 1, Q), F32),
        vm((2, 1, Q), F32),
        vm((2, 1, Q), F32),
        vm((Y, 2, 1, BLOCK), F32),
        vm((2, PAIR, Q), BF16),
        vm((2, BLOCK, Q), BF16),
        vm((2, 32, WIDTH), BF16),
        vm((2, 16, WIDTH), BF16),
        vm((ROWS + 64, WIDTH), F32),
        vm((ROWS + 32, WIDTH), F32),
        vm((Y, ROWS, WIDTH), BF16),
        vm((Y, ROWS, WIDTH), BF16),
        vm(block, BF16),
        vm((Y, Y, 8, BLOCK), F32),
        vm((Y, PAIR, BLOCK), BF16),
        vm((Y, PAIR, BLOCK), BF16),
        vm((2, ROWS, PAIR), BF16),
        vm((Y, WIDTH, PAIR), BF16),
        vm((Y, WIDTH, PAIR), BF16),
        vm((2, Z, ROWS // Z, PAIR), F32),
        vm((2, Z, ROWS // Z, PAIR), BF16),
        vm((2, Z, ROWS // Z, PAIR), BF16),
        vm((2, 2, 2, BLOCK, PAIR), F32),
        vm((2, Z // 2, 2, 2, ROWS, PAIR), BF16),
        vm((2, Z // 2, 2, 2, ROWS, PAIR), BF16),
        vm((3, 2, 2, ROWS, PAIR), BF16),
        vm((Y, 2, ROWS, PAIR), BF16),
        vm((Y, 2, ROWS, PAIR), BF16),
        vm((Y, crow, WIDTH), F32),
        vm((Y, crow, WIDTH), F32),
        vm((crow, WIDTH), F32),
        vm((crow, WIDTH), F32),
        vm((Z, crow, WIDTH), F32),
        vm((Y, crow, WIDTH), F32),
    ]
    semaphores = [
        (4,),
        (Y,),
        (5,),
        (6, Y),
        (2, Y, 2),
        (Z, 4),
        (2, Z // 2, 2, 2),
        (3, 2, 2),
        (2, Z),
        (Z,),
    ]
    for shape in semaphores:
        scratch += [dma(shape), dma(shape)]
    shapes = (
        jax.ShapeDtypeStruct(block, BF16),
        jax.ShapeDtypeStruct(block, BF16),
        jax.ShapeDtypeStruct(block, BF16),
        jax.ShapeDtypeStruct(block, BF16),
        jax.ShapeDtypeStruct((ROWS // Z, WIDTH), F32),
        jax.ShapeDtypeStruct((TAPS, WIDTH), F32),
    )
    results = pl.pallas_call(
        functools.partial(fused_kernel, Y, Z),
        out_shape=shapes,
        in_specs=[pl.BlockSpec(memory_space=pltpu.SMEM)] + [anywhere] * 6 + [vmem],
        out_specs=(anywhere,) * 6,
        scratch_shapes=scratch,
        compiler_params=pltpu.CompilerParams(
            collective_id=0, has_side_effects=True, vmem_limit_bytes=56 * 1024 * 1024
        ),
        name="conv_attention_backward",
    )(rec_lengths, query_all, key_all, value_all, cotangent, conv_input, out_proj, conv_weight)
    return pl.pallas_call(
        store_kernel, out_shape=shapes, in_specs=[vmem] * 6, out_specs=(vmem,) * 6, name="store_results"
    )(*results)


def solution(mesh):
    sizes = dict(mesh.shape)
    Y = sizes["head"]
    Z = sizes["ctx"] // (2 * Y)
    both = P("ctx", "head")
    return jax.shard_map(
        functools.partial(on_device, Y, Z),
        mesh=mesh,
        in_specs=(both, both, both, both, both, P(), P(None, "head"), P(None, "head")),
        out_specs=(both, both, both, both, both, P(None, "head")),
        check_vma=False,
    )
```

```python
import functools

import jax
import jax.numpy as jnp
from jax import lax
from jax.experimental import pallas as pl
from jax.experimental.pallas import tpu as pltpu
from jax.sharding import PartitionSpec as P

F32, BF16 = jnp.float32, jnp.bfloat16
HEAD_DIM = 64
ROWS = 128
WIDTH = 256
PAIR = 128
BLOCK = 256
TAPS = 31
NEG = -1e30
LOG2E = 1.4426950408889634
MESH = pl.DeviceIdType.MESH


def nt(a, b):
    return lax.dot_general(a, b, (((1,), (1,)), ((), ())), preferred_element_type=F32)


def tn(a, b):
    return lax.dot_general(a, b, (((0,), (0,)), ((), ())), preferred_element_type=F32)


def nn(a, b):
    return jnp.dot(a, b, preferred_element_type=F32)


def iota(shape, dim):
    return lax.broadcasted_iota(jnp.int32, shape, dim)


def fused_kernel(
    Y, Z,
    rec, q_in, k_in, v_in, ct_in, ci_in, w_in, taps,
    q_out, k_out, v_out, x_out, g_out, c_out,
    q, k, v, ct, ci, w, q_o, k_o, v_o, x_o, g_o, c_o, load_s, store_s,
    kv, qg, dog, kt, va, ka, vta, qta, probs, mk, mrun, ot, dot_, dqt, mst, lin, dlt, wts, gbuf, dsb,
    hci, hct, ext, gex, xf, xfp, do_s,
    st, os, orr, attn, gs, gr, gt, gz, gzr,
    part, rss, rsr, fin, dqs, dqr,
    cwp, cwr, c1, cx, cz, cfin,
    halo_s, halo_r, head_s, head_r, xs, xr, ys, yr, yxs, yxr, kvs, kvr, rs_s, rs_r, fin_s, fin_r, gzs, gzrs, czs, czr,
):
    Q = Y * BLOCK
    N = 2 * Y * Z
    HALF = Z // 2
    ctx, head = lax.axis_index("ctx"), lax.axis_index("head")
    y = lax.div(ctx, 2 * Z)
    xh = lax.rem(lax.div(ctx, Z), 2)
    z = lax.rem(ctx, Z)
    other = 1 - xh
    sides = (xh, other)

    def at(yy, xx, zz):
        return ((yy * 2 + xx) * Z + zz, head)

    def plus_y(d):
        return lax.rem(y + d, Y)

    def plus_z(d):
        return lax.rem(z + d, Z)

    def y_peer(d):
        return at(plus_y(d), xh, z)

    def z_peer(d):
        return at(y, xh, plus_z(d))

    def head_peer(d):
        return (ctx, lax.rem(head + d, Y))

    partner = at(y, other, z)
    following = (lax.rem(ctx + 1, N), head)
    preceding = (lax.rem(ctx + N - 1, N), head)

    def remote(src, dst, send, recv, device):
        return pltpu.make_async_remote_copy(
            src_ref=src, dst_ref=dst, send_sem=send, recv_sem=recv, device_id=device, device_id_type=MESH
        )

    own_cols = pl.ds(pl.multiple_of(xh * PAIR, PAIR), PAIR)
    other_cols = pl.ds(pl.multiple_of(other * PAIR, PAIR), PAIR)
    side_cols = (own_cols, other_cols)

    def halo(i):
        src, dst, dev = (
            (ci.at[pl.ds(ROWS - 32, 32)], hci.at[0], following),
            (ci.at[pl.ds(0, 32)], hci.at[1], preceding),
            (ct.at[pl.ds(ROWS - 16, 16)], hct.at[0], following),
            (ct.at[pl.ds(0, 16)], hct.at[1], preceding),
        )[i]
        return remote(src, dst, halo_s.at[i], halo_r.at[i], dev)

    XK, XV, XF, XCW = range(4)

    def x_copy(i):
        src, dst = (
            lambda: (k.at[:, other_cols], kv.at[0, 0, xh]),
            lambda: (v.at[:, other_cols], kv.at[0, 1, xh]),
            lambda: (xf, xfp),
            lambda: (c1, cx),
        )[i]()
        return remote(src, dst, xs.at[i], xr.at[i], partner)

    def x_recv(i):
        if i < XF:
            dst = kv.at[0, i, other]
            remote(dst, dst, xs.at[i], xr.at[i], partner).wait_recv()
        else:
            x_copy(i).wait_recv()

    YST, YO, YG, YC1, YC2 = range(5)

    def y_copy(i, d):
        src, dst = (
            lambda: (st.at[0], st.at[d]),
            lambda: (os.at[Y - d], orr.at[d]),
            lambda: (gs.at[plus_y(d)], gr.at[d]),
            lambda: (cwp.at[plus_y(d)], cwr.at[d]),
            lambda: (cfin.at[y], cfin.at[y]),
        )[i]()
        return remote(src, dst, ys.at[i, d], yr.at[i, d], y_peer(d))

    def y_start(i):
        for d in range(1, Y):
            y_copy(i, d).start()

    def y_recv(i):
        for d in range(1, Y):
            y_copy(i, d).wait_recv()

    spread = [(d, e) for d in range(Y) for e in range(2) if d or e]
    spread.sort(key=lambda pair: -min(pair[0], Y - pair[0]) - 2 * pair[1])
    SDO, SDQ, SQ = range(3)

    def spread_copy(i, d, e):
        src, dst = (
            lambda: (do_s.at[:, side_cols[e]], dog.at[d, xh]),
            lambda: (dqs.at[(Y - d) % Y, sides[e]], dqr.at[d, e]),
            lambda: (q.at[:, side_cols[e]], qg.at[d, xh]),
        )[i]()
        return remote(src, dst, yxs.at[i, d, e], yxr.at[i, d, e], at(plus_y(d), sides[e], z))

    def spread_recv(i):
        for d, e in spread:
            dst = (dog.at[d, sides[e]], dqr.at[d, e], qg.at[d, sides[e]])[i]
            remote(dst, dst, yxs.at[i, d, e], yxr.at[i, d, e], partner).wait_recv()

    def ring(src, dst, j, device):
        piece = (j % 2, sides[j // 2])
        return remote(kv.at[(src, *piece)], kv.at[(dst, *piece)], kvs.at[dst, j], kvr.at[dst, j], device)

    def ring_start(j):
        ring(0, 1, j, z_peer(1)).start()
        ring(0, Z - 1, j, z_peer(Z - 1)).start()

    def ring_event(level, j):
        ring(level, level, j, partner).wait_recv()

        @pl.when(level < HALF)
        def _():
            ring(level, level + 1, j, z_peer(1)).start()

        @pl.when(level < HALF)
        def _():
            ring(Z - level, Z - level, j, partner).wait_recv()

        @pl.when(level < HALF - 1)
        def _():
            ring(Z - level, Z - level - 1, j, z_peer(Z - 1)).start()

    shares = [(d, e) for d in range(Z) for e in range(2) if d or e]

    def gz_copy(d, e):
        return remote(
            gz.at[sides[e], plus_z(d)], gzr.at[e, d], gzs.at[e, d], gzrs.at[e, d], at(y, sides[e], plus_z(d))
        )

    def cz_copy(d):
        return remote(cz.at[z], cz.at[z], czs.at[d], czr.at[d], z_peer(d))

    loads = ((k_in, k), (v_in, v), (q_in, q), (ci_in, ci), (ct_in, ct), (None, None), (w_in, w))
    stores = ((x_o, x_out), (c_o, c_out), (g_o, g_out), (k_o, k_out), (v_o, v_out), (q_o, q_out))

    def load(i):
        return pltpu.make_async_copy(*loads[i], load_s.at[i])

    def store(i):
        return pltpu.make_async_copy(*stores[i], store_s.at[i])

    for i in (0, 1, 2, 3, 4, 6):
        load(i).start()
    peers = [partner, following, preceding, z_peer(1), z_peer(Z - 1)]
    peers += [at(plus_y(d), side, z) for d in range(1, Y) for side in sides]
    peers += [head_peer(d) for d in range(1, Y)]
    barrier = pltpu.get_barrier_semaphore()
    for peer in peers:
        pl.semaphore_signal(barrier, inc=1, device_id=peer, device_id_type=MESH)
    for i in range(5):
        load(i).wait()
    kv[0, 0, pl.ds(xh, 1)] = k[:, own_cols][None]
    kv[0, 1, pl.ds(xh, 1)] = v[:, own_cols][None]
    qg[0, pl.ds(xh, 1)] = q[:, own_cols][None]
    pl.semaphore_wait(barrier, len(peers))

    for i in range(4):
        halo(i).start()
    for i in (XK, XV):
        x_copy(i).start()
    for j in range(2):
        ring_start(j)
    for d, e in spread:
        spread_copy(SQ, d, e).start()
    valid = rec[0] + rec[1] + rec[2]

    for i in (0, 1):
        halo(i).wait_recv()
    pos = ctx * ROWS - 32 + iota((ROWS + 64, WIDTH), 0)
    ext[...] = jnp.where(
        (pos >= 0) & (pos < valid), jnp.concatenate([hci[0], ci[...], hci[1]], axis=0).astype(F32), 0.0
    )
    for i in (2, 3):
        halo(i).wait_recv()
    weights = taps[...].astype(F32)
    for c in range(2):
        cols = slice(c * 128, c * 128 + 128)
        conv = jnp.zeros((ROWS + 32, 128), F32)
        for b in range(8):
            moved = ext[b : b + ROWS + 56, cols]
            for a in range(4):
                j = 8 * a + b - 1
                if 0 <= j < TAPS:
                    conv = conv + weights[j : j + 1, cols] * moved[8 * a : 8 * a + ROWS + 32]
        sig = jax.nn.sigmoid(conv)
        up = jnp.concatenate([hct[0, :, cols], ct[:, cols], hct[1, :, cols]], axis=0).astype(F32)
        slope = (up * sig * (1.0 + conv * (1.0 - sig))).astype(BF16).astype(F32)
        gpos = ctx * ROWS - 16 + iota((ROWS + 32, 128), 0)
        gex[:, cols] = jnp.where((gpos >= 0) & (gpos < N * ROWS), slope, 0.0)

    for i, j in ((XK, 2), (XV, 3)):
        x_recv(i)
        ring_start(j)

    for c in range(2):
        cols = slice(c * 128, c * 128 + 128)
        back = jnp.zeros((ROWS, 128), F32)
        for b in range(8):
            moved = gex[b : b + ROWS + 24, cols]
            for a in range(4):
                j = TAPS - 8 * a - b
                if 0 <= j < TAPS:
                    back = back + weights[j : j + 1, cols] * moved[8 * a : 8 * a + ROWS]
        frame = ctx * ROWS + iota((ROWS, 128), 0)
        x16 = (ct[:, cols].astype(F32) + jnp.where(frame < valid, back, 0.0)).astype(BF16)
        x_o[:, cols] = x16
        xf[pl.ds(head, 1), :, cols] = x16[None]

    def head_copy(d, slot):
        return remote(xf.at[slot], xf.at[slot], head_s.at[d], head_r.at[d], head_peer(d))

    for d in [2, 1, 3] if Y == 4 else range(1, Y):
        head_copy(d, head).start()
    store(0).start()
    for j in range(4):
        ring_event(1, j)

    spread_recv(SQ)
    first_row = jnp.where(iota((16, BLOCK), 0) == 0, 1.0, 0.0).astype(BF16)
    zero_rows = jnp.zeros((112, BLOCK), BF16)
    for c in range(Y):
        cols = slice(c * BLOCK, (c + 1) * BLOCK)
        scaled = jnp.transpose(qg[c].reshape(BLOCK, PAIR).astype(F32) * (LOG2E * HEAD_DIM**-0.5))
        high = scaled.astype(BF16)
        low = (scaled - high.astype(F32)).astype(BF16)
        for h in range(2):
            rows = slice(h * HEAD_DIM, (h + 1) * HEAD_DIM)
            qta[h, :, cols] = jnp.concatenate([high[rows], low[rows], first_row, zero_rows], axis=0)

    ones_rows = jnp.ones((16, BLOCK), BF16)
    lane = iota((BLOCK, PAIR), 1)

    def prepare(slot, place):
        keys = kv[slot, 0].reshape(BLOCK, PAIR).astype(F32)
        values = kv[slot, 1].reshape(BLOCK, PAIR).astype(F32)
        values_t = jnp.transpose(values).astype(BF16)
        keys_moved = pltpu.roll(keys, HEAD_DIM, 1)
        origin = lax.rem(z + Z - slot, Z)
        row = iota((BLOCK, PAIR), 0)
        position = (y * 2 * Z + origin) * ROWS + lax.div(row, ROWS) * (Z * ROWS) + lax.rem(row, ROWS)
        bias = jnp.where((lane == 0) & (position >= valid), NEG, 0.0).astype(BF16)
        for h in range(2):
            first, second = (keys, keys_moved) if h == 0 else (keys_moved, keys)
            ka[place, h] = jnp.concatenate(
                [jnp.where(lane < HEAD_DIM, first, second).astype(BF16), bias], axis=1
            )
            vta[place, h] = jnp.concatenate([values_t[h * HEAD_DIM : (h + 1) * HEAD_DIM], ones_rows], axis=0)

    def forward_unit(slot, place, h):
        scores = nn(ka[place, h], qta[h])
        old = mrun[h]
        new = jnp.maximum(old, jnp.max(scores, axis=0, keepdims=True))
        p16 = jnp.exp2(scores - new).astype(BF16)
        probs[slot, h] = p16
        ot[h] = ot[h] * jnp.exp2(old - new) + nn(vta[place, h], p16)
        mrun[h] = new
        mk[slot, h] = new

    mrun[...] = jnp.full(mrun.shape, 2 * NEG, F32)
    ot[...] = jnp.zeros(ot.shape, F32)
    prepare(0, 0)
    for h in range(2):
        forward_unit(0, 0, h)

    crow = 32 // Y
    for c in range(2):
        cols = slice(c * 128, c * 128 + 128)
        grad = gex[16 : 16 + ROWS, cols]
        for b in range(8):
            moved = ext[b : b + ROWS + 40, cols]
            for a in range(2, 6):
                j = 8 * a + b - 17
                if 0 <= j < TAPS:
                    cwp[j // crow, j % crow : j % crow + 1, cols] = jnp.sum(
                        grad * moved[8 * a : 8 * a + ROWS], axis=0, keepdims=True
                    )
        cwp[Y - 1, crow - 1 : crow, cols] = jnp.zeros((1, 128), F32)
    y_start(YC1)

    for d in range(1, Y):
        head_copy(d, lax.rem(head + Y - d, Y)).wait_recv()
    load(6).wait()
    grad_out = jnp.zeros((ROWS, WIDTH), F32)
    for h in range(Y):
        grad_out = grad_out + nn(xf[h], w[h * WIDTH : (h + 1) * WIDTH, :])
    do_s[...] = grad_out.astype(BF16)
    for d, e in spread:
        spread_copy(SDO, d, e).start()
    dog[0, pl.ds(xh, 1)] = do_s[:, own_cols][None]
    x_copy(XF).start()

    def forward_step(d, carry):
        prepare(d, 0)

        @pl.when(d < HALF)
        def _():
            prepare(Z - d, 1)

        for j in range(4):

            @pl.when(d < HALF)
            def _():
                ring_event(d + 1, j)

            if j < 2:
                forward_unit(d, 0, j)
            else:

                @pl.when(d < HALF)
                def _():
                    forward_unit(Z - d, 1, j - 2)

        return carry

    lax.fori_loop(1, HALF + 1, forward_step, 0)

    spread_recv(SDO)
    for c in range(Y):
        cols = slice(c * BLOCK, (c + 1) * BLOCK)
        dot_[:, cols] = jnp.transpose(dog[c].reshape(BLOCK, PAIR).astype(F32))
        for h in range(2):
            out = ot[h, 0:HEAD_DIM, cols]
            total = ot[h, HEAD_DIM : HEAD_DIM + 1, cols]
            st[0, c, 3 * h : 3 * h + 1, :] = mrun[h, :, cols]
            st[0, c, 3 * h + 1 : 3 * h + 2, :] = total
            st[0, c, 3 * h + 2 : 3 * h + 3, :] = jnp.sum(
                out * dot_[h * HEAD_DIM : (h + 1) * HEAD_DIM, cols], axis=0, keepdims=True
            )
        st[0, c, 6:8, :] = jnp.zeros((2, BLOCK), F32)
    y_start(YST)
    for c in list(range(1, Y)) + [0]:
        cols = slice(c * BLOCK, (c + 1) * BLOCK)
        parts = [
            ot[h, 0:HEAD_DIM, cols] * (1.0 / ot[h, HEAD_DIM : HEAD_DIM + 1, cols]) for h in range(2)
        ]
        os[c] = jnp.concatenate(parts, axis=0).astype(BF16)
        if c:
            y_copy(YO, Y - c).start()

    y_recv(YC1)
    total = cwp[y]
    for d in range(1, Y):
        total = total + cwr[d]
    c1[...] = total
    x_copy(XCW).start()
    dqt[...] = jnp.zeros(dqt.shape, F32)

    def arrange(slot, carry):
        values = kv[slot, 1].reshape(BLOCK, PAIR).astype(F32)
        kt[slot] = jnp.transpose(kv[slot, 0].reshape(BLOCK, PAIR).astype(F32)).astype(BF16)
        extra = jnp.where(lane < HEAD_DIM + 2, 1.0, 0.0)
        for h, mine in enumerate((values, pltpu.roll(values, HEAD_DIM, 1))):
            va[slot, h] = jnp.where(lane < HEAD_DIM, mine, extra).astype(BF16)
        return carry

    lax.fori_loop(0, Z, arrange, 0)
    gbuf[...] = jnp.zeros(gbuf.shape, BF16)

    y_recv(YST)
    for c in range(Y):
        cols = slice(c * BLOCK, (c + 1) * BLOCK)
        rows = [st[e, (c - e) % Y] for e in range(Y)]
        for h in range(2):
            maxima = [r[3 * h : 3 * h + 1] for r in rows]
            top = functools.reduce(jnp.maximum, maxima)
            shrink = [jnp.exp2(m - top) for m in maxima]
            totals = [r[3 * h + 1 : 3 * h + 2] * f for r, f in zip(rows, shrink)]
            delta = sum(r[3 * h + 2 : 3 * h + 3] * f for r, f in zip(rows, shrink))
            inverse = 1.0 / sum(totals)
            mst[h, :, cols] = top
            lin[h, :, cols] = inverse
            dlt[h, :, cols] = delta * inverse
            if c == 0:
                for e in range(Y):
                    wts[e, h] = totals[e] * inverse

    delta_row = iota((16, Q), 0)

    def backward_unit(slot, place, parity, h):
        rows = slice(h * HEAD_DIM, (h + 1) * HEAD_DIM)
        factor = jnp.exp2(mk[slot, h] - mst[h]) * lin[h]
        shift = -dlt[h] * factor
        high = shift.astype(BF16).astype(F32)
        gbuf[h, 0:HEAD_DIM] = (dot_[rows] * factor).astype(BF16)
        gbuf[h, HEAD_DIM : HEAD_DIM + 16] = jnp.where(
            delta_row == 0, high, jnp.where(delta_row == 1, shift - high, 0.0)
        ).astype(BF16)
        slopes = nn(va[slot, h], gbuf[h])
        ds = (probs[slot, h].astype(F32) * slopes).astype(BF16)
        dsb[h] = ds
        dqt[rows] += nn(kt[slot, rows, :], ds)
        dk = nn(dsb[h], qg[...].reshape(Q, PAIR))
        part[place, parity, 0, :, rows] = dk[:, rows] * HEAD_DIM**-0.5
        part[place, parity, 1, :, rows] = nt(probs[slot, h], gbuf[h, 0:HEAD_DIM, :])

    def rs_copy(place, level, t, half, device):
        return remote(
            rss.at[place, level, t, half], rsr.at[place, level, t, half],
            rs_s.at[place, level, t, half], rs_r.at[place, level, t, half], device,
        )

    def fin_copy(kind, e, t, src):
        zz = (plus_z(1), plus_z(Z - 1), z)[kind]
        return remote(
            src, fin.at[kind, e, t], fin_s.at[kind, e, t], fin_r.at[kind, e, t], at(y, sides[e], zz)
        )

    def back_event(place, level, parity, j):
        t, half = j % 2, j // 2
        last = HALF - 1 - place
        rows = slice(half * ROWS, half * ROWS + ROWS)

        @pl.when(level > 0)
        def _():
            @pl.when(level <= last)
            def _():
                rs_copy(place, level - 1, t, half, partner).wait_recv()
                part[place, parity, t, rows] += rsr[place, level - 1, t, half].astype(F32)

        rss[place, level, t, half] = part[place, parity, t, rows].astype(BF16)

        @pl.when(level < last)
        def _():
            rs_copy(place, level, t, half, z_peer(1 if place == 0 else Z - 1)).start()

    def finish_event(place, level, kind):
        for e in range(2):
            for t in range(2):
                if kind < 2 or e == 1:
                    fin_copy(kind, e, t, rss.at[place, level, t, sides[e]]).start()

    for place in range(2):
        for h in range(2):
            backward_unit(HALF if place == 0 else HALF - 1, place, 0, h)
        for j in range(4):
            back_event(place, 0, 0, j)

    def backward_step(i, carry):
        parity = lax.rem(i, 2)
        ahead = 1 - parity

        for j in range(4):

            @pl.when(i > 0)
            def _():
                back_event(0, i, parity, j)
                back_event(1, i, parity, j)

            @pl.when(i < HALF - 1)
            def _():
                place, h = j // 2, j % 2
                backward_unit((HALF + 1 + i) if place == 0 else (HALF - 2 - i), place, ahead, h)

        @pl.when(i == HALF - 2)
        def _():
            finish_event(1, HALF - 2, 1)
            for c in sorted(range(Y), key=lambda c: -min(c, Y - c)):
                dqs[c] = (
                    jnp.transpose(dqt[:, c * BLOCK : (c + 1) * BLOCK] * HEAD_DIM**-0.5)
                    .astype(BF16)
                    .reshape(2, ROWS, PAIR)
                )
                for e in (1, 0):
                    if c or e:
                        spread_copy(SDQ, (Y - c) % Y, e).start()

        @pl.when(i == HALF - 1)
        def _():
            finish_event(1, HALF - 1, 2)
            finish_event(0, HALF - 1, 0)

        @pl.when(i == 0)
        def _():
            x_recv(XCW)
            cz[pl.ds(z, 1)] = (c1[...] + cx[...])[None]
            for d in range(1, Z):
                cz_copy(d).start()
            y_recv(YO)
            parts = []
            for h in range(2):
                rows = slice(h * HEAD_DIM, (h + 1) * HEAD_DIM)
                parts.append(
                    sum((os if e == 0 else orr)[e, rows, :].astype(F32) * wts[e, h] for e in range(Y))
                )
            attn[...] = jnp.transpose(jnp.concatenate(parts, axis=0)).astype(BF16).reshape(2, ROWS, PAIR)
            x_recv(XF)
            mine = attn[pl.ds(xh, 1)].reshape(ROWS, PAIR)
            theirs = attn[pl.ds(other, 1)].reshape(ROWS, PAIR)
            for h in range(Y):
                gs[h] = (tn(xf[h], mine) + tn(xfp[h], theirs)).astype(BF16)
            y_start(YG)

        @pl.when(i == min(2, HALF - 1))
        def _():
            y_recv(YG)
            sums = gs[pl.ds(y, 1)].reshape(WIDTH, PAIR).astype(F32)
            for d in range(1, Y):
                sums = sums + gr[d].astype(F32)
            sums = sums.reshape(2, Z, ROWS // Z, PAIR)
            gt[...] = sums
            gz[...] = sums.astype(BF16)
            for d, e in shares:
                gz_copy(d, e).start()
            for d in range(1, Z):
                slot = plus_z(Z - d)
                remote(cz.at[slot], cz.at[slot], czs.at[d], czr.at[d], partner).wait_recv()
            total = cz[0]
            for d in range(1, Z):
                total = total + cz[d]
            cfin[pl.ds(y, 1)] = total[None]
            y_start(YC2)

        return carry

    lax.fori_loop(0, HALF, backward_step, 0)

    for d in range(1, Y):
        slot = plus_y(Y - d)
        remote(cfin.at[slot], cfin.at[slot], ys.at[YC2, d], yr.at[YC2, d], partner).wait_recv()
    for h in range(Y):
        count = min(crow, TAPS - h * crow)
        c_o[h * crow : h * crow + count, :] = cfin[h, 0:count, :]
    store(1).start()

    for d, e in shares:
        gz_copy(d, e).wait_recv()
    for e in range(2):
        sums = gt[pl.ds(xh, 1), pl.ds(z, 1)].reshape(ROWS // Z, PAIR) if e == 0 else gzr[1, 0].astype(F32)
        for d in range(1, Z):
            sums = sums + gzr[e, d].astype(F32)
        g_o[:, side_cols[e]] = sums
    store(2).start()

    for t, out in ((0, k_o), (1, v_o)):
        for e in range(2):
            for kind in range(3):
                if kind < 2 or e == 1:
                    fin_copy(kind, e, t, fin.at[kind, e, t]).wait_recv()
            total = fin[0, e, t].astype(F32) + fin[1, e, t].astype(F32)
            if e == 0:
                start = pl.multiple_of(xh * ROWS, ROWS)
                total = total + part[1, (HALF - 1) % 2, t, pl.ds(start, ROWS), :]
            else:
                total = total + fin[2, 1, t].astype(F32)
            out[:, side_cols[e]] = total.astype(BF16)
        store(3 + t).start()

    spread_recv(SDQ)
    for e in range(2):
        total = dqs[0, pl.ds(xh, 1)].reshape(ROWS, PAIR).astype(F32) if e == 0 else dqr[0, 1].astype(F32)
        for d in range(1, Y):
            total = total + dqr[d, e].astype(F32)
        q_o[:, side_cols[e]] = total.astype(BF16)
    store(5).start()

    for i in range(4):
        halo(i).wait_send()
    for i in range(4):
        x_copy(i).wait_send()
    for i in range(5):
        for d in range(1, Y):
            y_copy(i, d).wait_send()
    for i in range(3):
        for d, e in spread:
            spread_copy(i, d, e).wait_send()
    for d in range(1, Y):
        head_copy(d, head).wait_send()
    for slot in range(1, Z):
        for j in range(4):
            ring(slot, slot, j, partner).wait_send()
    for t in range(2):
        for half in range(2):
            for level in range(HALF - 1):
                rs_copy(0, level, t, half, partner).wait_send()
            for level in range(HALF - 2):
                rs_copy(1, level, t, half, partner).wait_send()
        for e in range(2):
            for kind in range(3):
                if kind < 2 or e == 1:
                    fin_copy(kind, e, t, fin.at[kind, e, t]).wait_send()
    for d, e in shares:
        gz_copy(d, e).wait_send()
    for d in range(1, Z):
        cz_copy(d).wait_send()
    for i in range(6):
        store(i).wait()


def store_kernel(*refs):
    half = len(refs) // 2
    for source, target in zip(refs[:half], refs[half:]):
        target[...] = source[...]


def on_device(Y, Z, query_all, key_all, value_all, cotangent, conv_input, rec_lengths, out_proj, conv_weight):
    Q = Y * BLOCK
    vm, dma = pltpu.VMEM, pltpu.SemaphoreType.DMA
    vmem = pl.BlockSpec(memory_space=pltpu.VMEM)
    crow = 32 // Y
    block = (ROWS, WIDTH)
    anywhere = pl.BlockSpec(memory_space=pl.ANY)
    scratch = [vm(block, BF16) for name in ("q", "k", "v", "ct", "ci")]
    scratch += [vm((Y * WIDTH, WIDTH), BF16)]
    scratch += [vm(block, BF16) for name in ("q_o", "k_o", "v_o", "x_o")]
    scratch += [
        vm((ROWS // Z, WIDTH), F32),
        vm((TAPS, WIDTH), F32),
        dma((7,)),
        dma((6,)),
        vm((Z, 2, 2, ROWS, PAIR), BF16),
        vm((Y, 2, ROWS, PAIR), BF16),
        vm((Y, 2, ROWS, PAIR), BF16),
        vm((Z, PAIR, BLOCK), BF16),
        vm((Z, 2, BLOCK, PAIR), BF16),
        vm((2, 2, BLOCK, 2 * PAIR), BF16),
        vm((2, 2, HEAD_DIM + 16, BLOCK), BF16),
        vm((2, 2 * PAIR, Q), BF16),
        vm((Z, 2, BLOCK, Q), BF16),
        vm((Z, 2, 1, Q), F32),
        vm((2, 1, Q), F32),
        vm((2, HEAD_DIM + 16, Q), F32),
        vm((PAIR, Q), F32),
        vm((PAIR, Q), F32),
        vm((2, 1, Q), F32),
        vm((2, 1, Q), F32),
        vm((2, 1, Q), F32),
        vm((Y, 2, 1, BLOCK), F32),
        vm((2, PAIR, Q), BF16),
        vm((2, BLOCK, Q), BF16),
        vm((2, 32, WIDTH), BF16),
        vm((2, 16, WIDTH), BF16),
        vm((ROWS + 64, WIDTH), F32),
        vm((ROWS + 32, WIDTH), F32),
        vm((Y, ROWS, WIDTH), BF16),
        vm((Y, ROWS, WIDTH), BF16),
        vm(block, BF16),
        vm((Y, Y, 8, BLOCK), F32),
        vm((Y, PAIR, BLOCK), BF16),
        vm((Y, PAIR, BLOCK), BF16),
        vm((2, ROWS, PAIR), BF16),
        vm((Y, WIDTH, PAIR), BF16),
        vm((Y, WIDTH, PAIR), BF16),
        vm((2, Z, ROWS // Z, PAIR), F32),
        vm((2, Z, ROWS // Z, PAIR), BF16),
        vm((2, Z, ROWS // Z, PAIR), BF16),
        vm((2, 2, 2, BLOCK, PAIR), F32),
        vm((2, Z // 2, 2, 2, ROWS, PAIR), BF16),
        vm((2, Z // 2, 2, 2, ROWS, PAIR), BF16),
        vm((3, 2, 2, ROWS, PAIR), BF16),
        vm((Y, 2, ROWS, PAIR), BF16),
        vm((Y, 2, ROWS, PAIR), BF16),
        vm((Y, crow, WIDTH), F32),
        vm((Y, crow, WIDTH), F32),
        vm((crow, WIDTH), F32),
        vm((crow, WIDTH), F32),
        vm((Z, crow, WIDTH), F32),
        vm((Y, crow, WIDTH), F32),
    ]
    semaphores = [
        (4,),
        (Y,),
        (4,),
        (5, Y),
        (3, Y, 2),
        (Z, 4),
        (2, Z // 2, 2, 2),
        (3, 2, 2),
        (2, Z),
        (Z,),
    ]
    for shape in semaphores:
        scratch += [dma(shape), dma(shape)]
    shapes = (
        jax.ShapeDtypeStruct(block, BF16),
        jax.ShapeDtypeStruct(block, BF16),
        jax.ShapeDtypeStruct(block, BF16),
        jax.ShapeDtypeStruct(block, BF16),
        jax.ShapeDtypeStruct((ROWS // Z, WIDTH), F32),
        jax.ShapeDtypeStruct((TAPS, WIDTH), F32),
    )
    results = pl.pallas_call(
        functools.partial(fused_kernel, Y, Z),
        out_shape=shapes,
        in_specs=[pl.BlockSpec(memory_space=pltpu.SMEM)] + [anywhere] * 6 + [vmem],
        out_specs=(anywhere,) * 6,
        scratch_shapes=scratch,
        compiler_params=pltpu.CompilerParams(
            collective_id=0, has_side_effects=True, vmem_limit_bytes=56 * 1024 * 1024
        ),
        name="conv_attention_backward",
    )(rec_lengths, query_all, key_all, value_all, cotangent, conv_input, out_proj, conv_weight)
    return pl.pallas_call(
        store_kernel, out_shape=shapes, in_specs=[vmem] * 6, out_specs=(vmem,) * 6, name="store_results"
    )(*results)


def solution(mesh):
    sizes = dict(mesh.shape)
    Y = sizes["head"]
    Z = sizes["ctx"] // (2 * Y)
    both = P("ctx", "head")
    return jax.shard_map(
        functools.partial(on_device, Y, Z),
        mesh=mesh,
        in_specs=(both, both, both, both, both, P(), P(None, "head"), P(None, "head")),
        out_specs=(both, both, both, both, both, P(None, "head")),
        check_vma=False,
    )
```

```python
import functools

import jax
import jax.numpy as jnp
from jax import lax
from jax.experimental import pallas as pl
from jax.experimental.pallas import tpu as pltpu
from jax.sharding import PartitionSpec as P

F32, BF16 = jnp.float32, jnp.bfloat16
HEAD_DIM = 64
ROWS = 128
WIDTH = 256
PAIR = 128
BLOCK = 256
TAPS = 31
NEG = -1e30
LOG2E = 1.4426950408889634
MESH = pl.DeviceIdType.MESH


def nt(a, b):
    return lax.dot_general(a, b, (((1,), (1,)), ((), ())), preferred_element_type=F32)


def tn(a, b):
    return lax.dot_general(a, b, (((0,), (0,)), ((), ())), preferred_element_type=F32)


def nn(a, b):
    return jnp.dot(a, b, preferred_element_type=F32)


def iota(shape, dim):
    return lax.broadcasted_iota(jnp.int32, shape, dim)


def fused_kernel(
    Y, Z,
    rec, q_in, k_in, v_in, ct_in, ci_in, w_in, taps,
    q_out, k_out, v_out, x_out, g_out, c_out,
    q, k, v, ct, ci, w, q_o, k_o, v_o, x_o, g_o, c_o, load_s, store_s,
    kv, qg, dog, kt, va, ka, vta, qta, probs, mk, mrun, ot, dot_, dqt, mst, lin, dlt, wts, gbuf, dsb,
    hci, hct, ext, gex, xf, xfp, do_s,
    st, os, orr, attn, gs, gr, gt, gz, gzr,
    part, rss, rsr, fin, dqs, dqr,
    cwp, cwr, c1, cx, cz, cfin,
    halo_s, halo_r, head_s, head_r, xs, xr, ys, yr, yxs, yxr, kvs, kvr, rs_s, rs_r, fin_s, fin_r, gzs, gzrs, czs, czr,
):
    Q = Y * BLOCK
    N = 2 * Y * Z
    HALF = Z // 2
    ctx, head = lax.axis_index("ctx"), lax.axis_index("head")
    y = lax.div(ctx, 2 * Z)
    xh = lax.rem(lax.div(ctx, Z), 2)
    z = lax.rem(ctx, Z)
    other = 1 - xh
    sides = (xh, other)

    def at(yy, xx, zz):
        return ((yy * 2 + xx) * Z + zz, head)

    def plus_y(d):
        return lax.rem(y + d, Y)

    def plus_z(d):
        return lax.rem(z + d, Z)

    def y_peer(d):
        return at(plus_y(d), xh, z)

    def z_peer(d):
        return at(y, xh, plus_z(d))

    def head_peer(d):
        return (ctx, lax.rem(head + d, Y))

    partner = at(y, other, z)
    following = (lax.rem(ctx + 1, N), head)
    preceding = (lax.rem(ctx + N - 1, N), head)

    def remote(src, dst, send, recv, device):
        return pltpu.make_async_remote_copy(
            src_ref=src, dst_ref=dst, send_sem=send, recv_sem=recv, device_id=device, device_id_type=MESH
        )

    own_cols = pl.ds(pl.multiple_of(xh * PAIR, PAIR), PAIR)
    other_cols = pl.ds(pl.multiple_of(other * PAIR, PAIR), PAIR)
    side_cols = (own_cols, other_cols)

    def halo(i):
        src, dst, dev = (
            (ci.at[pl.ds(ROWS - 32, 32)], hci.at[0], following),
            (ci.at[pl.ds(0, 32)], hci.at[1], preceding),
            (ct.at[pl.ds(ROWS - 16, 16)], hct.at[0], following),
            (ct.at[pl.ds(0, 16)], hct.at[1], preceding),
        )[i]
        return remote(src, dst, halo_s.at[i], halo_r.at[i], dev)

    XK, XV, XF, XCW = range(4)

    def x_copy(i):
        src, dst = (
            lambda: (k.at[:, other_cols], kv.at[0, 0, xh]),
            lambda: (v.at[:, other_cols], kv.at[0, 1, xh]),
            lambda: (xf, xfp),
            lambda: (c1, cx),
        )[i]()
        return remote(src, dst, xs.at[i], xr.at[i], partner)

    def x_recv(i):
        if i < XF:
            dst = kv.at[0, i, other]
            remote(dst, dst, xs.at[i], xr.at[i], partner).wait_recv()
        else:
            x_copy(i).wait_recv()

    YST, YO, YG, YC1, YC2 = range(5)

    def y_copy(i, d):
        src, dst = (
            lambda: (st.at[0], st.at[d]),
            lambda: (os.at[Y - d], orr.at[d]),
            lambda: (gs.at[plus_y(d)], gr.at[d]),
            lambda: (cwp.at[plus_y(d)], cwr.at[d]),
            lambda: (cfin.at[y], cfin.at[y]),
        )[i]()
        return remote(src, dst, ys.at[i, d], yr.at[i, d], y_peer(d))

    def y_start(i):
        for d in range(1, Y):
            y_copy(i, d).start()

    def y_recv(i):
        for d in range(1, Y):
            y_copy(i, d).wait_recv()

    spread = [(d, e) for d in range(Y) for e in range(2) if d or e]
    spread.sort(key=lambda pair: -min(pair[0], Y - pair[0]) - 2 * pair[1])
    SDO, SDQ, SQ = range(3)

    def spread_copy(i, d, e):
        src, dst = (
            lambda: (do_s.at[:, side_cols[e]], dog.at[d, xh]),
            lambda: (dqs.at[(Y - d) % Y, sides[e]], dqr.at[d, e]),
            lambda: (q.at[:, side_cols[e]], qg.at[d, xh]),
        )[i]()
        return remote(src, dst, yxs.at[i, d, e], yxr.at[i, d, e], at(plus_y(d), sides[e], z))

    def spread_recv(i):
        for d, e in spread:
            dst = (dog.at[d, sides[e]], dqr.at[d, e], qg.at[d, sides[e]])[i]
            remote(dst, dst, yxs.at[i, d, e], yxr.at[i, d, e], partner).wait_recv()

    def ring(src, dst, j, device):
        piece = (j % 2, sides[j // 2])
        return remote(kv.at[(src, *piece)], kv.at[(dst, *piece)], kvs.at[dst, j], kvr.at[dst, j], device)

    def ring_start(j):
        ring(0, 1, j, z_peer(1)).start()
        ring(0, Z - 1, j, z_peer(Z - 1)).start()

    def ring_event(level, j):
        ring(level, level, j, partner).wait_recv()

        @pl.when(level < HALF)
        def _():
            ring(level, level + 1, j, z_peer(1)).start()

        @pl.when(level < HALF)
        def _():
            ring(Z - level, Z - level, j, partner).wait_recv()

        @pl.when(level < HALF - 1)
        def _():
            ring(Z - level, Z - level - 1, j, z_peer(Z - 1)).start()

    shares = [(d, e) for d in range(Z) for e in range(2) if d or e]

    def gz_copy(d, e):
        return remote(
            gz.at[sides[e], plus_z(d)], gzr.at[e, d], gzs.at[e, d], gzrs.at[e, d], at(y, sides[e], plus_z(d))
        )

    def cz_copy(d):
        return remote(cz.at[z], cz.at[z], czs.at[d], czr.at[d], z_peer(d))

    loads = ((k_in, k), (v_in, v), (q_in, q), (ci_in, ci), (ct_in, ct), (None, None), (w_in, w))
    stores = ((x_o, x_out), (c_o, c_out), (g_o, g_out), (k_o, k_out), (v_o, v_out), (q_o, q_out))

    def load(i):
        return pltpu.make_async_copy(*loads[i], load_s.at[i])

    def store(i):
        return pltpu.make_async_copy(*stores[i], store_s.at[i])

    for i in (0, 1, 2, 3, 4, 6):
        load(i).start()
    peers = [partner, following, preceding, z_peer(1), z_peer(Z - 1)]
    peers += [at(plus_y(d), side, z) for d in range(1, Y) for side in sides]
    peers += [head_peer(d) for d in range(1, Y)]
    barrier = pltpu.get_barrier_semaphore()
    for peer in peers:
        pl.semaphore_signal(barrier, inc=1, device_id=peer, device_id_type=MESH)
    for i in range(5):
        load(i).wait()
    kv[0, 0, pl.ds(xh, 1)] = k[:, own_cols][None]
    kv[0, 1, pl.ds(xh, 1)] = v[:, own_cols][None]
    qg[0, pl.ds(xh, 1)] = q[:, own_cols][None]
    pl.semaphore_wait(barrier, len(peers))

    for i in range(4):
        halo(i).start()
    for i in (XK, XV):
        x_copy(i).start()
    for j in range(2):
        ring_start(j)
    for d, e in spread:
        spread_copy(SQ, d, e).start()
    valid = rec[0] + rec[1] + rec[2]

    for i in (0, 1):
        halo(i).wait_recv()
    pos = ctx * ROWS - 32 + iota((ROWS + 64, WIDTH), 0)
    ext[...] = jnp.where(
        (pos >= 0) & (pos < valid), jnp.concatenate([hci[0], ci[...], hci[1]], axis=0).astype(F32), 0.0
    )
    for i in (2, 3):
        halo(i).wait_recv()
    weights = taps[...].astype(F32)
    for c in range(2):
        cols = slice(c * 128, c * 128 + 128)
        conv = jnp.zeros((ROWS + 32, 128), F32)
        for b in range(8):
            moved = ext[b : b + ROWS + 56, cols]
            for a in range(4):
                j = 8 * a + b - 1
                if 0 <= j < TAPS:
                    conv = conv + weights[j : j + 1, cols] * moved[8 * a : 8 * a + ROWS + 32]
        sig = jax.nn.sigmoid(conv)
        up = jnp.concatenate([hct[0, :, cols], ct[:, cols], hct[1, :, cols]], axis=0).astype(F32)
        slope = (up * sig * (1.0 + conv * (1.0 - sig))).astype(BF16).astype(F32)
        gpos = ctx * ROWS - 16 + iota((ROWS + 32, 128), 0)
        gex[:, cols] = jnp.where((gpos >= 0) & (gpos < N * ROWS), slope, 0.0)

    for i, j in ((XK, 2), (XV, 3)):
        x_recv(i)
        ring_start(j)

    for c in range(2):
        cols = slice(c * 128, c * 128 + 128)
        back = jnp.zeros((ROWS, 128), F32)
        for b in range(8):
            moved = gex[b : b + ROWS + 24, cols]
            for a in range(4):
                j = TAPS - 8 * a - b
                if 0 <= j < TAPS:
                    back = back + weights[j : j + 1, cols] * moved[8 * a : 8 * a + ROWS]
        frame = ctx * ROWS + iota((ROWS, 128), 0)
        x16 = (ct[:, cols].astype(F32) + jnp.where(frame < valid, back, 0.0)).astype(BF16)
        x_o[:, cols] = x16
        xf[pl.ds(head, 1), :, cols] = x16[None]

    def head_copy(d, slot):
        return remote(xf.at[slot], xf.at[slot], head_s.at[d], head_r.at[d], head_peer(d))

    for d in [2, 1, 3] if Y == 4 else range(1, Y):
        head_copy(d, head).start()
    store(0).start()
    for j in range(4):
        ring_event(1, j)

    spread_recv(SQ)
    first_row = jnp.where(iota((16, BLOCK), 0) == 0, 1.0, 0.0).astype(BF16)
    zero_rows = jnp.zeros((112, BLOCK), BF16)
    for c in range(Y):
        cols = slice(c * BLOCK, (c + 1) * BLOCK)
        scaled = jnp.transpose(qg[c].reshape(BLOCK, PAIR).astype(F32) * (LOG2E * HEAD_DIM**-0.5))
        high = scaled.astype(BF16)
        low = (scaled - high.astype(F32)).astype(BF16)
        for h in range(2):
            rows = slice(h * HEAD_DIM, (h + 1) * HEAD_DIM)
            qta[h, :, cols] = jnp.concatenate([high[rows], low[rows], first_row, zero_rows], axis=0)

    ones_rows = jnp.ones((16, BLOCK), BF16)
    lane = iota((BLOCK, PAIR), 1)

    def prepare(slot, place):
        keys = kv[slot, 0].reshape(BLOCK, PAIR).astype(F32)
        values = kv[slot, 1].reshape(BLOCK, PAIR).astype(F32)
        values_t = jnp.transpose(values).astype(BF16)
        keys_moved = pltpu.roll(keys, HEAD_DIM, 1)
        origin = lax.rem(z + Z - slot, Z)
        row = iota((BLOCK, PAIR), 0)
        position = (y * 2 * Z + origin) * ROWS + lax.div(row, ROWS) * (Z * ROWS) + lax.rem(row, ROWS)
        bias = jnp.where((lane == 0) & (position >= valid), NEG, 0.0).astype(BF16)
        for h in range(2):
            first, second = (keys, keys_moved) if h == 0 else (keys_moved, keys)
            ka[place, h] = jnp.concatenate(
                [jnp.where(lane < HEAD_DIM, first, second).astype(BF16), bias], axis=1
            )
            vta[place, h] = jnp.concatenate([values_t[h * HEAD_DIM : (h + 1) * HEAD_DIM], ones_rows], axis=0)

    def forward_unit(slot, place, h):
        scores = nn(ka[place, h], qta[h])
        old = mrun[h]
        new = jnp.maximum(old, jnp.max(scores, axis=0, keepdims=True))
        p16 = jnp.exp2(scores - new).astype(BF16)
        probs[slot, h] = p16
        ot[h] = ot[h] * jnp.exp2(old - new) + nn(vta[place, h], p16)
        mrun[h] = new
        mk[slot, h] = new

    mrun[...] = jnp.full(mrun.shape, 2 * NEG, F32)
    ot[...] = jnp.zeros(ot.shape, F32)
    prepare(0, 0)
    for h in range(2):
        forward_unit(0, 0, h)

    crow = 32 // Y
    for c in range(2):
        cols = slice(c * 128, c * 128 + 128)
        grad = gex[16 : 16 + ROWS, cols]
        for b in range(8):
            moved = ext[b : b + ROWS + 40, cols]
            for a in range(2, 6):
                j = 8 * a + b - 17
                if 0 <= j < TAPS:
                    cwp[j // crow, j % crow : j % crow + 1, cols] = jnp.sum(
                        grad * moved[8 * a : 8 * a + ROWS], axis=0, keepdims=True
                    )
        cwp[Y - 1, crow - 1 : crow, cols] = jnp.zeros((1, 128), F32)
    y_start(YC1)

    for d in range(1, Y):
        head_copy(d, lax.rem(head + Y - d, Y)).wait_recv()
    load(6).wait()
    grad_out = jnp.zeros((ROWS, WIDTH), F32)
    for h in range(Y):
        grad_out = grad_out + nn(xf[h], w[h * WIDTH : (h + 1) * WIDTH, :])
    do_s[...] = grad_out.astype(BF16)
    for d, e in spread:
        spread_copy(SDO, d, e).start()
    dog[0, pl.ds(xh, 1)] = do_s[:, own_cols][None]
    x_copy(XF).start()

    def forward_step(d, carry):
        prepare(d, 0)

        @pl.when(d < HALF)
        def _():
            prepare(Z - d, 1)

        for j in range(4):

            @pl.when(d < HALF)
            def _():
                ring_event(d + 1, j)

            if j < 2:
                forward_unit(d, 0, j)
            else:

                @pl.when(d < HALF)
                def _():
                    forward_unit(Z - d, 1, j - 2)

        return carry

    lax.fori_loop(1, HALF + 1, forward_step, 0)

    spread_recv(SDO)
    for c in range(Y):
        cols = slice(c * BLOCK, (c + 1) * BLOCK)
        dot_[:, cols] = jnp.transpose(dog[c].reshape(BLOCK, PAIR).astype(F32))
        for h in range(2):
            out = ot[h, 0:HEAD_DIM, cols]
            total = ot[h, HEAD_DIM : HEAD_DIM + 1, cols]
            st[0, c, 3 * h : 3 * h + 1, :] = mrun[h, :, cols]
            st[0, c, 3 * h + 1 : 3 * h + 2, :] = total
            st[0, c, 3 * h + 2 : 3 * h + 3, :] = jnp.sum(
                out * dot_[h * HEAD_DIM : (h + 1) * HEAD_DIM, cols], axis=0, keepdims=True
            )
        st[0, c, 6:8, :] = jnp.zeros((2, BLOCK), F32)
    y_start(YST)
    for c in list(range(1, Y)) + [0]:
        cols = slice(c * BLOCK, (c + 1) * BLOCK)
        parts = [
            ot[h, 0:HEAD_DIM, cols] * (1.0 / ot[h, HEAD_DIM : HEAD_DIM + 1, cols]) for h in range(2)
        ]
        os[c] = jnp.concatenate(parts, axis=0).astype(BF16)
        if c:
            y_copy(YO, Y - c).start()

    y_recv(YC1)
    total = cwp[y]
    for d in range(1, Y):
        total = total + cwr[d]
    c1[...] = total
    x_copy(XCW).start()
    dqt[...] = jnp.zeros(dqt.shape, F32)

    def arrange(slot, carry):
        values = kv[slot, 1].reshape(BLOCK, PAIR).astype(F32)
        kt[slot] = jnp.transpose(kv[slot, 0].reshape(BLOCK, PAIR).astype(F32)).astype(BF16)
        extra = jnp.where(lane < HEAD_DIM + 2, 1.0, 0.0)
        for h, mine in enumerate((values, pltpu.roll(values, HEAD_DIM, 1))):
            va[slot, h] = jnp.where(lane < HEAD_DIM, mine, extra).astype(BF16)
        return carry

    lax.fori_loop(0, Z, arrange, 0)
    gbuf[...] = jnp.zeros(gbuf.shape, BF16)

    y_recv(YST)
    for c in range(Y):
        cols = slice(c * BLOCK, (c + 1) * BLOCK)
        rows = [st[e, (c - e) % Y] for e in range(Y)]
        for h in range(2):
            maxima = [r[3 * h : 3 * h + 1] for r in rows]
            top = functools.reduce(jnp.maximum, maxima)
            shrink = [jnp.exp2(m - top) for m in maxima]
            totals = [r[3 * h + 1 : 3 * h + 2] * f for r, f in zip(rows, shrink)]
            delta = sum(r[3 * h + 2 : 3 * h + 3] * f for r, f in zip(rows, shrink))
            inverse = 1.0 / sum(totals)
            mst[h, :, cols] = top
            lin[h, :, cols] = inverse
            dlt[h, :, cols] = delta * inverse
            if c == 0:
                for e in range(Y):
                    wts[e, h] = totals[e] * inverse

    delta_row = iota((16, Q), 0)

    def backward_unit(slot, place, parity, h):
        rows = slice(h * HEAD_DIM, (h + 1) * HEAD_DIM)
        factor = jnp.exp2(mk[slot, h] - mst[h]) * lin[h]
        shift = -dlt[h] * factor
        high = shift.astype(BF16).astype(F32)
        gbuf[h, 0:HEAD_DIM] = (dot_[rows] * factor).astype(BF16)
        gbuf[h, HEAD_DIM : HEAD_DIM + 16] = jnp.where(
            delta_row == 0, high, jnp.where(delta_row == 1, shift - high, 0.0)
        ).astype(BF16)
        slopes = nn(va[slot, h], gbuf[h])
        ds = (probs[slot, h].astype(F32) * slopes).astype(BF16)
        dsb[h] = ds
        dqt[rows] += nn(kt[slot, rows, :], ds)
        dk = nn(dsb[h], qg[...].reshape(Q, PAIR))
        part[place, parity, 0, :, rows] = dk[:, rows] * HEAD_DIM**-0.5
        part[place, parity, 1, :, rows] = nt(probs[slot, h], gbuf[h, 0:HEAD_DIM, :])

    def rs_copy(place, level, t, half, device):
        return remote(
            rss.at[place, level, t, half], rsr.at[place, level, t, half],
            rs_s.at[place, level, t, half], rs_r.at[place, level, t, half], device,
        )

    def fin_copy(kind, e, t, src):
        zz = (plus_z(1), z)[kind]
        return remote(
            src, fin.at[kind, e, t], fin_s.at[kind, e, t], fin_r.at[kind, e, t], at(y, sides[e], zz)
        )

    def back_event(place, level, parity, j):
        t, e = j % 2, 1 - j // 2
        half = sides[e]
        last = HALF - 1
        rows = pl.ds(pl.multiple_of(half * ROWS, ROWS), ROWS)

        @pl.when(level > 0)
        def _():
            rs_copy(place, level - 1, t, half, partner).wait_recv()
            part[place, parity, t, rows] += rsr[place, level - 1, t, half].astype(F32)

        rss[place, level, t, half] = part[place, parity, t, rows].astype(BF16)

        @pl.when(level < last)
        def _():
            rs_copy(place, level, t, half, z_peer(1 if place == 0 else Z - 1)).start()

        if place == 0 or e == 1:

            @pl.when(level == last)
            def _():
                fin_copy(place, e, t, rss.at[place, level, t, half]).start()

    for place in range(2):
        for h in range(2):
            backward_unit(HALF if place == 0 else HALF - 1, place, 0, h)
        for j in range(4):
            back_event(place, 0, 0, j)

    def backward_step(i, carry):
        parity = lax.rem(i, 2)
        ahead = 1 - parity

        for j in range(4):

            @pl.when(i > 0)
            def _():
                back_event(0, i, parity, j)
                back_event(1, i, parity, j)

            @pl.when(i < HALF - 1)
            def _():
                place, h = j // 2, j % 2
                backward_unit((HALF + 1 + i) if place == 0 else (HALF - 2 - i), place, ahead, h)

        @pl.when(i == HALF - 2)
        def _():
            for c in sorted(range(Y), key=lambda c: -min(c, Y - c)):
                dqs[c] = (
                    jnp.transpose(dqt[:, c * BLOCK : (c + 1) * BLOCK] * HEAD_DIM**-0.5)
                    .astype(BF16)
                    .reshape(2, ROWS, PAIR)
                )
                for e in (1, 0):
                    if c or e:
                        spread_copy(SDQ, (Y - c) % Y, e).start()

        @pl.when(i == 0)
        def _():
            x_recv(XCW)
            cz[pl.ds(z, 1)] = (c1[...] + cx[...])[None]
            for d in range(1, Z):
                cz_copy(d).start()
            y_recv(YO)
            parts = []
            for h in range(2):
                rows = slice(h * HEAD_DIM, (h + 1) * HEAD_DIM)
                parts.append(
                    sum((os if e == 0 else orr)[e, rows, :].astype(F32) * wts[e, h] for e in range(Y))
                )
            attn[...] = jnp.transpose(jnp.concatenate(parts, axis=0)).astype(BF16).reshape(2, ROWS, PAIR)
            x_recv(XF)
            mine = attn[pl.ds(xh, 1)].reshape(ROWS, PAIR)
            theirs = attn[pl.ds(other, 1)].reshape(ROWS, PAIR)
            for h in range(Y):
                gs[h] = (tn(xf[h], mine) + tn(xfp[h], theirs)).astype(BF16)
            y_start(YG)

        @pl.when(i == min(2, HALF - 1))
        def _():
            y_recv(YG)
            sums = gs[pl.ds(y, 1)].reshape(WIDTH, PAIR).astype(F32)
            for d in range(1, Y):
                sums = sums + gr[d].astype(F32)
            sums = sums.reshape(2, Z, ROWS // Z, PAIR)
            gt[...] = sums
            gz[...] = sums.astype(BF16)
            for d, e in shares:
                gz_copy(d, e).start()
            for d in range(1, Z):
                slot = plus_z(Z - d)
                remote(cz.at[slot], cz.at[slot], czs.at[d], czr.at[d], partner).wait_recv()
            total = cz[0]
            for d in range(1, Z):
                total = total + cz[d]
            cfin[pl.ds(y, 1)] = total[None]
            y_start(YC2)

        return carry

    lax.fori_loop(0, HALF, backward_step, 0)

    for d in range(1, Y):
        slot = plus_y(Y - d)
        remote(cfin.at[slot], cfin.at[slot], ys.at[YC2, d], yr.at[YC2, d], partner).wait_recv()
    for h in range(Y):
        count = min(crow, TAPS - h * crow)
        c_o[h * crow : h * crow + count, :] = cfin[h, 0:count, :]
    store(1).start()

    for d, e in shares:
        gz_copy(d, e).wait_recv()
    for e in range(2):
        sums = gt[pl.ds(xh, 1), pl.ds(z, 1)].reshape(ROWS // Z, PAIR) if e == 0 else gzr[1, 0].astype(F32)
        for d in range(1, Z):
            sums = sums + gzr[e, d].astype(F32)
        g_o[:, side_cols[e]] = sums
    store(2).start()

    for t, out in ((0, k_o), (1, v_o)):
        for e in range(2):
            for kind in range(1 + e):
                fin_copy(kind, e, t, fin.at[kind, e, t]).wait_recv()
            total = fin[0, e, t].astype(F32)
            if e == 0:
                start = pl.multiple_of(xh * ROWS, ROWS)
                total = total + part[1, (HALF - 1) % 2, t, pl.ds(start, ROWS), :]
            else:
                total = total + fin[1, 1, t].astype(F32)
            out[:, side_cols[e]] = total.astype(BF16)
        store(3 + t).start()

    spread_recv(SDQ)
    for e in range(2):
        total = dqs[0, pl.ds(xh, 1)].reshape(ROWS, PAIR).astype(F32) if e == 0 else dqr[0, 1].astype(F32)
        for d in range(1, Y):
            total = total + dqr[d, e].astype(F32)
        q_o[:, side_cols[e]] = total.astype(BF16)
    store(5).start()

    for i in range(4):
        halo(i).wait_send()
    for i in range(4):
        x_copy(i).wait_send()
    for i in range(5):
        for d in range(1, Y):
            y_copy(i, d).wait_send()
    for i in range(3):
        for d, e in spread:
            spread_copy(i, d, e).wait_send()
    for d in range(1, Y):
        head_copy(d, head).wait_send()
    for slot in range(1, Z):
        for j in range(4):
            ring(slot, slot, j, partner).wait_send()
    for t in range(2):
        for half in range(2):
            for level in range(HALF - 1):
                for place in range(2):
                    rs_copy(place, level, t, half, partner).wait_send()
        for e in range(2):
            for kind in range(1 + e):
                fin_copy(kind, e, t, fin.at[kind, e, t]).wait_send()
    for d, e in shares:
        gz_copy(d, e).wait_send()
    for d in range(1, Z):
        cz_copy(d).wait_send()
    for i in range(6):
        store(i).wait()


def store_kernel(*refs):
    half = len(refs) // 2
    for source, target in zip(refs[:half], refs[half:]):
        target[...] = source[...]


def on_device(Y, Z, query_all, key_all, value_all, cotangent, conv_input, rec_lengths, out_proj, conv_weight):
    Q = Y * BLOCK
    vm, dma = pltpu.VMEM, pltpu.SemaphoreType.DMA
    vmem = pl.BlockSpec(memory_space=pltpu.VMEM)
    crow = 32 // Y
    block = (ROWS, WIDTH)
    anywhere = pl.BlockSpec(memory_space=pl.ANY)
    scratch = [vm(block, BF16) for name in ("q", "k", "v", "ct", "ci")]
    scratch += [vm((Y * WIDTH, WIDTH), BF16)]
    scratch += [vm(block, BF16) for name in ("q_o", "k_o", "v_o", "x_o")]
    scratch += [
        vm((ROWS // Z, WIDTH), F32),
        vm((TAPS, WIDTH), F32),
        dma((7,)),
        dma((6,)),
        vm((Z, 2, 2, ROWS, PAIR), BF16),
        vm((Y, 2, ROWS, PAIR), BF16),
        vm((Y, 2, ROWS, PAIR), BF16),
        vm((Z, PAIR, BLOCK), BF16),
        vm((Z, 2, BLOCK, PAIR), BF16),
        vm((2, 2, BLOCK, 2 * PAIR), BF16),
        vm((2, 2, HEAD_DIM + 16, BLOCK), BF16),
        vm((2, 2 * PAIR, Q), BF16),
        vm((Z, 2, BLOCK, Q), BF16),
        vm((Z, 2, 1, Q), F32),
        vm((2, 1, Q), F32),
        vm((2, HEAD_DIM + 16, Q), F32),
        vm((PAIR, Q), F32),
        vm((PAIR, Q), F32),
        vm((2, 1, Q), F32),
        vm((2, 1, Q), F32),
        vm((2, 1, Q), F32),
        vm((Y, 2, 1, BLOCK), F32),
        vm((2, PAIR, Q), BF16),
        vm((2, BLOCK, Q), BF16),
        vm((2, 32, WIDTH), BF16),
        vm((2, 16, WIDTH), BF16),
        vm((ROWS + 64, WIDTH), F32),
        vm((ROWS + 32, WIDTH), F32),
        vm((Y, ROWS, WIDTH), BF16),
        vm((Y, ROWS, WIDTH), BF16),
        vm(block, BF16),
        vm((Y, Y, 8, BLOCK), F32),
        vm((Y, PAIR, BLOCK), BF16),
        vm((Y, PAIR, BLOCK), BF16),
        vm((2, ROWS, PAIR), BF16),
        vm((Y, WIDTH, PAIR), BF16),
        vm((Y, WIDTH, PAIR), BF16),
        vm((2, Z, ROWS // Z, PAIR), F32),
        vm((2, Z, ROWS // Z, PAIR), BF16),
        vm((2, Z, ROWS // Z, PAIR), BF16),
        vm((2, 2, 2, BLOCK, PAIR), F32),
        vm((2, Z // 2, 2, 2, ROWS, PAIR), BF16),
        vm((2, Z // 2, 2, 2, ROWS, PAIR), BF16),
        vm((2, 2, 2, ROWS, PAIR), BF16),
        vm((Y, 2, ROWS, PAIR), BF16),
        vm((Y, 2, ROWS, PAIR), BF16),
        vm((Y, crow, WIDTH), F32),
        vm((Y, crow, WIDTH), F32),
        vm((crow, WIDTH), F32),
        vm((crow, WIDTH), F32),
        vm((Z, crow, WIDTH), F32),
        vm((Y, crow, WIDTH), F32),
    ]
    semaphores = [
        (4,),
        (Y,),
        (4,),
        (5, Y),
        (3, Y, 2),
        (Z, 4),
        (2, Z // 2, 2, 2),
        (2, 2, 2),
        (2, Z),
        (Z,),
    ]
    for shape in semaphores:
        scratch += [dma(shape), dma(shape)]
    shapes = (
        jax.ShapeDtypeStruct(block, BF16),
        jax.ShapeDtypeStruct(block, BF16),
        jax.ShapeDtypeStruct(block, BF16),
        jax.ShapeDtypeStruct(block, BF16),
        jax.ShapeDtypeStruct((ROWS // Z, WIDTH), F32),
        jax.ShapeDtypeStruct((TAPS, WIDTH), F32),
    )
    results = pl.pallas_call(
        functools.partial(fused_kernel, Y, Z),
        out_shape=shapes,
        in_specs=[pl.BlockSpec(memory_space=pltpu.SMEM)] + [anywhere] * 6 + [vmem],
        out_specs=(anywhere,) * 6,
        scratch_shapes=scratch,
        compiler_params=pltpu.CompilerParams(
            collective_id=0, has_side_effects=True, vmem_limit_bytes=56 * 1024 * 1024
        ),
        name="conv_attention_backward",
    )(rec_lengths, query_all, key_all, value_all, cotangent, conv_input, out_proj, conv_weight)
    return pl.pallas_call(
        store_kernel, out_shape=shapes, in_specs=[vmem] * 6, out_specs=(vmem,) * 6, name="store_results"
    )(*results)


def solution(mesh):
    sizes = dict(mesh.shape)
    Y = sizes["head"]
    Z = sizes["ctx"] // (2 * Y)
    both = P("ctx", "head")
    return jax.shard_map(
        functools.partial(on_device, Y, Z),
        mesh=mesh,
        in_specs=(both, both, both, both, both, P(), P(None, "head"), P(None, "head")),
        out_specs=(both, both, both, both, both, P(None, "head")),
        check_vma=False,
    )
```

```python
import functools

import jax
import jax.numpy as jnp
from jax import lax
from jax.experimental import pallas as pl
from jax.experimental.pallas import tpu as pltpu
from jax.sharding import PartitionSpec as P

F32, BF16 = jnp.float32, jnp.bfloat16
HEAD_DIM = 64
ROWS = 128
WIDTH = 256
PAIR = 128
BLOCK = 256
TAPS = 31
NEG = -1e30
LOG2E = 1.4426950408889634
MESH = pl.DeviceIdType.MESH


def nt(a, b):
    return lax.dot_general(a, b, (((1,), (1,)), ((), ())), preferred_element_type=F32)


def tn(a, b):
    return lax.dot_general(a, b, (((0,), (0,)), ((), ())), preferred_element_type=F32)


def nn(a, b):
    return jnp.dot(a, b, preferred_element_type=F32)


def iota(shape, dim):
    return lax.broadcasted_iota(jnp.int32, shape, dim)


def fused_kernel(
    Y, Z,
    rec, q_in, k_in, v_in, ct_in, ci_in, w_in, taps,
    q_out, k_out, v_out, x_out, g_out, c_out,
    q, k, v, ct, ci, w, q_o, k_o, v_o, x_o, g_o, c_o, load_s, store_s,
    kv, qg, dog, kt, va, ka, vta, qta, probs, mk, mrun, ot, dot_, dqt, mst, lin, dlt, wts, gbuf, dsb,
    hci, hct, ext, gex, xf, xfp, do_s,
    st, os, orr, attn, gs, gr, gt, gz, gzr,
    part, rss, rsr, fin, dqs, dqr,
    cwp, cwr, c1, cx, cz, cfin,
    halo_s, halo_r, head_s, head_r, xs, xr, ys, yr, yxs, yxr, kvs, kvr, rs_s, rs_r, fin_s, fin_r, gzs, gzrs, czs, czr,
):
    Q = Y * BLOCK
    N = 2 * Y * Z
    HALF = Z // 2
    ctx, head = lax.axis_index("ctx"), lax.axis_index("head")
    y = lax.div(ctx, 2 * Z)
    xh = lax.rem(lax.div(ctx, Z), 2)
    z = lax.rem(ctx, Z)
    other = 1 - xh
    sides = (xh, other)

    def at(yy, xx, zz):
        return ((yy * 2 + xx) * Z + zz, head)

    def plus_y(d):
        return lax.rem(y + d, Y)

    def plus_z(d):
        return lax.rem(z + d, Z)

    def y_peer(d):
        return at(plus_y(d), xh, z)

    def z_peer(d):
        return at(y, xh, plus_z(d))

    def head_peer(d):
        return (ctx, lax.rem(head + d, Y))

    partner = at(y, other, z)
    following = (lax.rem(ctx + 1, N), head)
    preceding = (lax.rem(ctx + N - 1, N), head)

    def remote(src, dst, send, recv, device):
        return pltpu.make_async_remote_copy(
            src_ref=src, dst_ref=dst, send_sem=send, recv_sem=recv, device_id=device, device_id_type=MESH
        )

    own_cols = pl.ds(pl.multiple_of(xh * PAIR, PAIR), PAIR)
    other_cols = pl.ds(pl.multiple_of(other * PAIR, PAIR), PAIR)
    side_cols = (own_cols, other_cols)

    def halo(i):
        src, dst, dev = (
            (ci.at[pl.ds(ROWS - 32, 32)], hci.at[0], following),
            (ci.at[pl.ds(0, 32)], hci.at[1], preceding),
            (ct.at[pl.ds(ROWS - 16, 16)], hct.at[0], following),
            (ct.at[pl.ds(0, 16)], hct.at[1], preceding),
        )[i]
        return remote(src, dst, halo_s.at[i], halo_r.at[i], dev)

    XK, XV, XF, XCW = range(4)

    def x_copy(i):
        src, dst = (
            lambda: (k.at[:, other_cols], kv.at[0, 0, xh]),
            lambda: (v.at[:, other_cols], kv.at[0, 1, xh]),
            lambda: (xf, xfp),
            lambda: (c1, cx),
        )[i]()
        return remote(src, dst, xs.at[i], xr.at[i], partner)

    def x_recv(i):
        if i < XF:
            dst = kv.at[0, i, other]
            remote(dst, dst, xs.at[i], xr.at[i], partner).wait_recv()
        else:
            x_copy(i).wait_recv()

    YST, YO, YG, YC1, YC2 = range(5)

    def y_copy(i, d):
        src, dst = (
            lambda: (st.at[0], st.at[d]),
            lambda: (os.at[Y - d], orr.at[d]),
            lambda: (gs.at[plus_y(d)], gr.at[d]),
            lambda: (cwp.at[plus_y(d)], cwr.at[d]),
            lambda: (cfin.at[y], cfin.at[y]),
        )[i]()
        return remote(src, dst, ys.at[i, d], yr.at[i, d], y_peer(d))

    def y_start(i):
        for d in range(1, Y):
            y_copy(i, d).start()

    def y_recv(i):
        for d in range(1, Y):
            y_copy(i, d).wait_recv()

    spread = [(d, e) for d in range(Y) for e in range(2) if d or e]
    spread.sort(key=lambda pair: -min(pair[0], Y - pair[0]) - 2 * pair[1])
    SDO, SDQ, SQ = range(3)

    def spread_copy(i, d, e):
        src, dst = (
            lambda: (do_s.at[:, side_cols[e]], dog.at[d, xh]),
            lambda: (dqs.at[(Y - d) % Y, sides[e]], dqr.at[d, e]),
            lambda: (q.at[:, side_cols[e]], qg.at[d, xh]),
        )[i]()
        return remote(src, dst, yxs.at[i, d, e], yxr.at[i, d, e], at(plus_y(d), sides[e], z))

    def spread_recv(i):
        for d, e in spread:
            dst = (dog.at[d, sides[e]], dqr.at[d, e], qg.at[d, sides[e]])[i]
            remote(dst, dst, yxs.at[i, d, e], yxr.at[i, d, e], partner).wait_recv()

    def ring(src, dst, j, device):
        piece = (j % 2, sides[j // 2])
        return remote(kv.at[(src, *piece)], kv.at[(dst, *piece)], kvs.at[dst, j], kvr.at[dst, j], device)

    def ring_start(j):
        ring(0, 1, j, z_peer(1)).start()
        ring(0, Z - 1, j, z_peer(Z - 1)).start()

    def ring_event(level, j):
        ring(level, level, j, partner).wait_recv()

        @pl.when(level < HALF)
        def _():
            ring(level, level + 1, j, z_peer(1)).start()

        @pl.when(level < HALF)
        def _():
            ring(Z - level, Z - level, j, partner).wait_recv()

        @pl.when(level < HALF - 1)
        def _():
            ring(Z - level, Z - level - 1, j, z_peer(Z - 1)).start()

    shares = [(d, e) for d in range(Z) for e in range(2) if d or e]

    def gz_copy(d, e):
        return remote(
            gz.at[sides[e], plus_z(d)], gzr.at[e, d], gzs.at[e, d], gzrs.at[e, d], at(y, sides[e], plus_z(d))
        )

    def cz_copy(d):
        return remote(cz.at[z], cz.at[z], czs.at[d], czr.at[d], z_peer(d))

    loads = ((k_in, k), (v_in, v), (q_in, q), (ci_in, ci), (ct_in, ct), (None, None), (w_in, w))
    stores = ((x_o, x_out), (c_o, c_out), (g_o, g_out), (k_o, k_out), (v_o, v_out), (q_o, q_out))

    def load(i):
        return pltpu.make_async_copy(*loads[i], load_s.at[i])

    def store(i):
        return pltpu.make_async_copy(*stores[i], store_s.at[i])

    for i in (0, 1, 2, 3, 4, 6):
        load(i).start()
    peers = [partner, following, preceding, z_peer(1), z_peer(Z - 1)]
    peers += [at(plus_y(d), side, z) for d in range(1, Y) for side in sides]
    peers += [head_peer(d) for d in range(1, Y)]
    barrier = pltpu.get_barrier_semaphore()
    for peer in peers:
        pl.semaphore_signal(barrier, inc=1, device_id=peer, device_id_type=MESH)
    for i in range(5):
        load(i).wait()
    kv[0, 0, pl.ds(xh, 1)] = k[:, own_cols][None]
    kv[0, 1, pl.ds(xh, 1)] = v[:, own_cols][None]
    qg[0, pl.ds(xh, 1)] = q[:, own_cols][None]
    pl.semaphore_wait(barrier, len(peers))

    for i in range(4):
        halo(i).start()
    for i in (XK, XV):
        x_copy(i).start()
    for j in range(2):
        ring_start(j)
    for d, e in spread:
        spread_copy(SQ, d, e).start()
    valid = rec[0] + rec[1] + rec[2]

    for i in (0, 1):
        halo(i).wait_recv()
    pos = ctx * ROWS - 32 + iota((ROWS + 64, WIDTH), 0)
    ext[...] = jnp.where(
        (pos >= 0) & (pos < valid), jnp.concatenate([hci[0], ci[...], hci[1]], axis=0).astype(F32), 0.0
    )
    for i in (2, 3):
        halo(i).wait_recv()
    weights = taps[...].astype(F32)
    for c in range(2):
        cols = slice(c * 128, c * 128 + 128)
        conv = jnp.zeros((ROWS + 32, 128), F32)
        for b in range(8):
            moved = ext[b : b + ROWS + 56, cols]
            for a in range(4):
                j = 8 * a + b - 1
                if 0 <= j < TAPS:
                    conv = conv + weights[j : j + 1, cols] * moved[8 * a : 8 * a + ROWS + 32]
        sig = jax.nn.sigmoid(conv)
        up = jnp.concatenate([hct[0, :, cols], ct[:, cols], hct[1, :, cols]], axis=0).astype(F32)
        slope = (up * sig * (1.0 + conv * (1.0 - sig))).astype(BF16).astype(F32)
        gpos = ctx * ROWS - 16 + iota((ROWS + 32, 128), 0)
        gex[:, cols] = jnp.where((gpos >= 0) & (gpos < N * ROWS), slope, 0.0)

    for i, j in ((XK, 2), (XV, 3)):
        x_recv(i)
        ring_start(j)

    for c in range(2):
        cols = slice(c * 128, c * 128 + 128)
        back = jnp.zeros((ROWS, 128), F32)
        for b in range(8):
            moved = gex[b : b + ROWS + 24, cols]
            for a in range(4):
                j = TAPS - 8 * a - b
                if 0 <= j < TAPS:
                    back = back + weights[j : j + 1, cols] * moved[8 * a : 8 * a + ROWS]
        frame = ctx * ROWS + iota((ROWS, 128), 0)
        x16 = (ct[:, cols].astype(F32) + jnp.where(frame < valid, back, 0.0)).astype(BF16)
        x_o[:, cols] = x16
        xf[pl.ds(head, 1), :, cols] = x16[None]

    def head_copy(d, slot):
        return remote(xf.at[slot], xf.at[slot], head_s.at[d], head_r.at[d], head_peer(d))

    for d in [2, 1, 3] if Y == 4 else range(1, Y):
        head_copy(d, head).start()
    store(0).start()
    for j in range(4):
        ring_event(1, j)

    spread_recv(SQ)
    first_row = jnp.where(iota((16, BLOCK), 0) == 0, 1.0, 0.0).astype(BF16)
    zero_rows = jnp.zeros((112, BLOCK), BF16)
    for c in range(Y):
        cols = slice(c * BLOCK, (c + 1) * BLOCK)
        scaled = jnp.transpose(qg[c].reshape(BLOCK, PAIR).astype(F32) * (LOG2E * HEAD_DIM**-0.5))
        high = scaled.astype(BF16)
        low = (scaled - high.astype(F32)).astype(BF16)
        for h in range(2):
            rows = slice(h * HEAD_DIM, (h + 1) * HEAD_DIM)
            qta[h, :, cols] = jnp.concatenate([high[rows], low[rows], first_row, zero_rows], axis=0)

    ones_rows = jnp.ones((16, BLOCK), BF16)
    lane = iota((BLOCK, PAIR), 1)

    def prepare(slot, place):
        keys = kv[slot, 0].reshape(BLOCK, PAIR).astype(F32)
        values = kv[slot, 1].reshape(BLOCK, PAIR).astype(F32)
        values_t = jnp.transpose(values).astype(BF16)
        keys_moved = pltpu.roll(keys, HEAD_DIM, 1)
        origin = lax.rem(z + Z - slot, Z)
        row = iota((BLOCK, PAIR), 0)
        position = (y * 2 * Z + origin) * ROWS + lax.div(row, ROWS) * (Z * ROWS) + lax.rem(row, ROWS)
        bias = jnp.where((lane == 0) & (position >= valid), NEG, 0.0).astype(BF16)
        for h in range(2):
            first, second = (keys, keys_moved) if h == 0 else (keys_moved, keys)
            ka[place, h] = jnp.concatenate(
                [jnp.where(lane < HEAD_DIM, first, second).astype(BF16), bias], axis=1
            )
            vta[place, h] = jnp.concatenate([values_t[h * HEAD_DIM : (h + 1) * HEAD_DIM], ones_rows], axis=0)

    def forward_unit(slot, place, h):
        scores = nn(ka[place, h], qta[h])
        old = mrun[h]
        new = jnp.maximum(old, jnp.max(scores, axis=0, keepdims=True))
        p16 = jnp.exp2(scores - new).astype(BF16)
        probs[slot, h] = p16
        ot[h] = ot[h] * jnp.exp2(old - new) + nn(vta[place, h], p16)
        mrun[h] = new
        mk[slot, h] = new

    mrun[...] = jnp.full(mrun.shape, 2 * NEG, F32)
    ot[...] = jnp.zeros(ot.shape, F32)
    prepare(0, 0)
    for h in range(2):
        forward_unit(0, 0, h)

    crow = 32 // Y
    for c in range(2):
        cols = slice(c * 128, c * 128 + 128)
        grad = gex[16 : 16 + ROWS, cols]
        for b in range(8):
            moved = ext[b : b + ROWS + 40, cols]
            for a in range(2, 6):
                j = 8 * a + b - 17
                if 0 <= j < TAPS:
                    cwp[j // crow, j % crow : j % crow + 1, cols] = jnp.sum(
                        grad * moved[8 * a : 8 * a + ROWS], axis=0, keepdims=True
                    )
        cwp[Y - 1, crow - 1 : crow, cols] = jnp.zeros((1, 128), F32)
    y_start(YC1)

    for d in range(1, Y):
        head_copy(d, lax.rem(head + Y - d, Y)).wait_recv()
    load(6).wait()
    grad_out = jnp.zeros((ROWS, WIDTH), F32)
    for h in range(Y):
        grad_out = grad_out + nn(xf[h], w[h * WIDTH : (h + 1) * WIDTH, :])
    do_s[...] = grad_out.astype(BF16)
    for d, e in spread:
        spread_copy(SDO, d, e).start()
    dog[0, pl.ds(xh, 1)] = do_s[:, own_cols][None]
    x_copy(XF).start()

    def forward_step(d, carry):
        prepare(d, 0)

        @pl.when(d < HALF)
        def _():
            prepare(Z - d, 1)

        for j in range(4):

            @pl.when(d < HALF)
            def _():
                ring_event(d + 1, j)

            if j < 2:
                forward_unit(d, 0, j)
            else:

                @pl.when(d < HALF)
                def _():
                    forward_unit(Z - d, 1, j - 2)

        return carry

    lax.fori_loop(1, HALF + 1, forward_step, 0)

    spread_recv(SDO)
    for c in range(Y):
        cols = slice(c * BLOCK, (c + 1) * BLOCK)
        dot_[:, cols] = jnp.transpose(dog[c].reshape(BLOCK, PAIR).astype(F32))
        for h in range(2):
            out = ot[h, 0:HEAD_DIM, cols]
            total = ot[h, HEAD_DIM : HEAD_DIM + 1, cols]
            st[0, c, 3 * h : 3 * h + 1, :] = mrun[h, :, cols]
            st[0, c, 3 * h + 1 : 3 * h + 2, :] = total
            st[0, c, 3 * h + 2 : 3 * h + 3, :] = jnp.sum(
                out * dot_[h * HEAD_DIM : (h + 1) * HEAD_DIM, cols], axis=0, keepdims=True
            )
        st[0, c, 6:8, :] = jnp.zeros((2, BLOCK), F32)
    y_start(YST)
    for c in list(range(1, Y)) + [0]:
        cols = slice(c * BLOCK, (c + 1) * BLOCK)
        parts = [
            ot[h, 0:HEAD_DIM, cols] * (1.0 / ot[h, HEAD_DIM : HEAD_DIM + 1, cols]) for h in range(2)
        ]
        os[c] = jnp.concatenate(parts, axis=0).astype(BF16)
        if c:
            y_copy(YO, Y - c).start()

    y_recv(YC1)
    total = cwp[y]
    for d in range(1, Y):
        total = total + cwr[d]
    c1[...] = total
    x_copy(XCW).start()
    dqt[...] = jnp.zeros(dqt.shape, F32)

    def arrange(slot, carry):
        values = kv[slot, 1].reshape(BLOCK, PAIR).astype(F32)
        kt[slot] = jnp.transpose(kv[slot, 0].reshape(BLOCK, PAIR).astype(F32)).astype(BF16)
        extra = jnp.where(lane < HEAD_DIM + 2, 1.0, 0.0)
        for h, mine in enumerate((values, pltpu.roll(values, HEAD_DIM, 1))):
            va[slot, h] = jnp.where(lane < HEAD_DIM, mine, extra).astype(BF16)
        return carry

    lax.fori_loop(0, Z, arrange, 0)
    gbuf[...] = jnp.zeros(gbuf.shape, BF16)

    y_recv(YST)
    for c in range(Y):
        cols = slice(c * BLOCK, (c + 1) * BLOCK)
        rows = [st[e, (c - e) % Y] for e in range(Y)]
        for h in range(2):
            maxima = [r[3 * h : 3 * h + 1] for r in rows]
            top = functools.reduce(jnp.maximum, maxima)
            shrink = [jnp.exp2(m - top) for m in maxima]
            totals = [r[3 * h + 1 : 3 * h + 2] * f for r, f in zip(rows, shrink)]
            delta = sum(r[3 * h + 2 : 3 * h + 3] * f for r, f in zip(rows, shrink))
            inverse = 1.0 / sum(totals)
            mst[h, :, cols] = top
            lin[h, :, cols] = inverse
            dlt[h, :, cols] = delta * inverse
            if c == 0:
                for e in range(Y):
                    wts[e, h] = totals[e] * inverse

    delta_row = iota((16, Q), 0)

    def backward_unit(slot, place, parity, h):
        rows = slice(h * HEAD_DIM, (h + 1) * HEAD_DIM)
        factor = jnp.exp2(mk[slot, h] - mst[h]) * lin[h]
        shift = -dlt[h] * factor
        high = shift.astype(BF16).astype(F32)
        gbuf[h, 0:HEAD_DIM] = (dot_[rows] * factor).astype(BF16)
        gbuf[h, HEAD_DIM : HEAD_DIM + 16] = jnp.where(
            delta_row == 0, high, jnp.where(delta_row == 1, shift - high, 0.0)
        ).astype(BF16)
        slopes = nn(va[slot, h], gbuf[h])
        ds = (probs[slot, h].astype(F32) * slopes).astype(BF16)
        dsb[h] = ds
        dqt[rows] += nn(kt[slot, rows, :], ds)
        dk = nn(dsb[h], qg[...].reshape(Q, PAIR))
        part[place, parity, 0, :, rows] = dk[:, rows] * HEAD_DIM**-0.5
        part[place, parity, 1, :, rows] = nt(probs[slot, h], gbuf[h, 0:HEAD_DIM, :])

    def rs_copy(place, level, t, half, device):
        return remote(
            rss.at[place, level, t, half], rsr.at[place, level, t, half],
            rs_s.at[place, level, t, half], rs_r.at[place, level, t, half], device,
        )

    def fin_copy(kind, e, t, src):
        zz = (plus_z(1), z)[kind]
        return remote(
            src, fin.at[kind, e, t], fin_s.at[kind, e, t], fin_r.at[kind, e, t], at(y, sides[e], zz)
        )

    def back_event(place, level, parity, j):
        t, e = j % 2, 1 - j // 2
        half = sides[e]
        last = HALF - 1
        rows = pl.ds(pl.multiple_of(half * ROWS, ROWS), ROWS)

        @pl.when(level > 0)
        def _():
            rs_copy(place, level - 1, t, half, partner).wait_recv()
            part[place, parity, t, rows] += rsr[place, level - 1, t, half].astype(F32)

        rss[place, level, t, half] = part[place, parity, t, rows].astype(BF16)

        @pl.when(level < last)
        def _():
            rs_copy(place, level, t, half, z_peer(1 if place == 0 else Z - 1)).start()

        if place == 0 or e == 1:

            @pl.when(level == last)
            def _():
                fin_copy(place, e, t, rss.at[place, level, t, half]).start()

    for place in range(2):
        for h in range(2):
            backward_unit(HALF if place == 0 else HALF - 1, place, 0, h)
        for j in range(4):
            back_event(place, 0, 0, j)

    def backward_step(i, carry):
        parity = lax.rem(i, 2)
        ahead = 1 - parity

        for j in range(4):

            @pl.when(i > 0)
            def _():
                for piece in ((0, 1), (2, 3), (), ())[j]:
                    back_event(0, i, parity, piece)
                    back_event(1, i, parity, piece)

            @pl.when(i < HALF - 1)
            def _():
                place, h = j // 2, j % 2
                backward_unit((HALF + 1 + i) if place == 0 else (HALF - 2 - i), place, ahead, h)

        @pl.when(i == HALF - 2)
        def _():
            for c in sorted(range(Y), key=lambda c: -min(c, Y - c)):
                dqs[c] = (
                    jnp.transpose(dqt[:, c * BLOCK : (c + 1) * BLOCK] * HEAD_DIM**-0.5)
                    .astype(BF16)
                    .reshape(2, ROWS, PAIR)
                )
                for e in (1, 0):
                    if c or e:
                        spread_copy(SDQ, (Y - c) % Y, e).start()

        @pl.when(i == 0)
        def _():
            x_recv(XCW)
            cz[pl.ds(z, 1)] = (c1[...] + cx[...])[None]
            for d in range(1, Z):
                cz_copy(d).start()
            y_recv(YO)
            parts = []
            for h in range(2):
                rows = slice(h * HEAD_DIM, (h + 1) * HEAD_DIM)
                parts.append(
                    sum((os if e == 0 else orr)[e, rows, :].astype(F32) * wts[e, h] for e in range(Y))
                )
            attn[...] = jnp.transpose(jnp.concatenate(parts, axis=0)).astype(BF16).reshape(2, ROWS, PAIR)
            x_recv(XF)
            mine = attn[pl.ds(xh, 1)].reshape(ROWS, PAIR)
            theirs = attn[pl.ds(other, 1)].reshape(ROWS, PAIR)
            for h in range(Y):
                gs[h] = (tn(xf[h], mine) + tn(xfp[h], theirs)).astype(BF16)
            y_start(YG)

        @pl.when(i == min(2, HALF - 1))
        def _():
            y_recv(YG)
            sums = gs[pl.ds(y, 1)].reshape(WIDTH, PAIR).astype(F32)
            for d in range(1, Y):
                sums = sums + gr[d].astype(F32)
            sums = sums.reshape(2, Z, ROWS // Z, PAIR)
            gt[...] = sums
            gz[...] = sums.astype(BF16)
            for d, e in shares:
                gz_copy(d, e).start()
            for d in range(1, Z):
                slot = plus_z(Z - d)
                remote(cz.at[slot], cz.at[slot], czs.at[d], czr.at[d], partner).wait_recv()
            total = cz[0]
            for d in range(1, Z):
                total = total + cz[d]
            cfin[pl.ds(y, 1)] = total[None]
            y_start(YC2)

        return carry

    lax.fori_loop(0, HALF, backward_step, 0)

    for d in range(1, Y):
        slot = plus_y(Y - d)
        remote(cfin.at[slot], cfin.at[slot], ys.at[YC2, d], yr.at[YC2, d], partner).wait_recv()
    for h in range(Y):
        count = min(crow, TAPS - h * crow)
        c_o[h * crow : h * crow + count, :] = cfin[h, 0:count, :]
    store(1).start()

    for d, e in shares:
        gz_copy(d, e).wait_recv()
    for e in range(2):
        sums = gt[pl.ds(xh, 1), pl.ds(z, 1)].reshape(ROWS // Z, PAIR) if e == 0 else gzr[1, 0].astype(F32)
        for d in range(1, Z):
            sums = sums + gzr[e, d].astype(F32)
        g_o[:, side_cols[e]] = sums
    store(2).start()

    for t, out in ((0, k_o), (1, v_o)):
        for e in range(2):
            for kind in range(1 + e):
                fin_copy(kind, e, t, fin.at[kind, e, t]).wait_recv()
            total = fin[0, e, t].astype(F32)
            if e == 0:
                start = pl.multiple_of(xh * ROWS, ROWS)
                total = total + part[1, (HALF - 1) % 2, t, pl.ds(start, ROWS), :]
            else:
                total = total + fin[1, 1, t].astype(F32)
            out[:, side_cols[e]] = total.astype(BF16)
        store(3 + t).start()

    spread_recv(SDQ)
    for e in range(2):
        total = dqs[0, pl.ds(xh, 1)].reshape(ROWS, PAIR).astype(F32) if e == 0 else dqr[0, 1].astype(F32)
        for d in range(1, Y):
            total = total + dqr[d, e].astype(F32)
        q_o[:, side_cols[e]] = total.astype(BF16)
    store(5).start()

    for i in range(4):
        halo(i).wait_send()
    for i in range(4):
        x_copy(i).wait_send()
    for i in range(5):
        for d in range(1, Y):
            y_copy(i, d).wait_send()
    for i in range(3):
        for d, e in spread:
            spread_copy(i, d, e).wait_send()
    for d in range(1, Y):
        head_copy(d, head).wait_send()
    for slot in range(1, Z):
        for j in range(4):
            ring(slot, slot, j, partner).wait_send()
    for t in range(2):
        for half in range(2):
            for level in range(HALF - 1):
                for place in range(2):
                    rs_copy(place, level, t, half, partner).wait_send()
        for e in range(2):
            for kind in range(1 + e):
                fin_copy(kind, e, t, fin.at[kind, e, t]).wait_send()
    for d, e in shares:
        gz_copy(d, e).wait_send()
    for d in range(1, Z):
        cz_copy(d).wait_send()
    for i in range(6):
        store(i).wait()


def store_kernel(*refs):
    half = len(refs) // 2
    for source, target in zip(refs[:half], refs[half:]):
        target[...] = source[...]


def on_device(Y, Z, query_all, key_all, value_all, cotangent, conv_input, rec_lengths, out_proj, conv_weight):
    Q = Y * BLOCK
    vm, dma = pltpu.VMEM, pltpu.SemaphoreType.DMA
    vmem = pl.BlockSpec(memory_space=pltpu.VMEM)
    crow = 32 // Y
    block = (ROWS, WIDTH)
    anywhere = pl.BlockSpec(memory_space=pl.ANY)
    scratch = [vm(block, BF16) for name in ("q", "k", "v", "ct", "ci")]
    scratch += [vm((Y * WIDTH, WIDTH), BF16)]
    scratch += [vm(block, BF16) for name in ("q_o", "k_o", "v_o", "x_o")]
    scratch += [
        vm((ROWS // Z, WIDTH), F32),
        vm((TAPS, WIDTH), F32),
        dma((7,)),
        dma((6,)),
        vm((Z, 2, 2, ROWS, PAIR), BF16),
        vm((Y, 2, ROWS, PAIR), BF16),
        vm((Y, 2, ROWS, PAIR), BF16),
        vm((Z, PAIR, BLOCK), BF16),
        vm((Z, 2, BLOCK, PAIR), BF16),
        vm((2, 2, BLOCK, 2 * PAIR), BF16),
        vm((2, 2, HEAD_DIM + 16, BLOCK), BF16),
        vm((2, 2 * PAIR, Q), BF16),
        vm((Z, 2, BLOCK, Q), BF16),
        vm((Z, 2, 1, Q), F32),
        vm((2, 1, Q), F32),
        vm((2, HEAD_DIM + 16, Q), F32),
        vm((PAIR, Q), F32),
        vm((PAIR, Q), F32),
        vm((2, 1, Q), F32),
        vm((2, 1, Q), F32),
        vm((2, 1, Q), F32),
        vm((Y, 2, 1, BLOCK), F32),
        vm((2, PAIR, Q), BF16),
        vm((2, BLOCK, Q), BF16),
        vm((2, 32, WIDTH), BF16),
        vm((2, 16, WIDTH), BF16),
        vm((ROWS + 64, WIDTH), F32),
        vm((ROWS + 32, WIDTH), F32),
        vm((Y, ROWS, WIDTH), BF16),
        vm((Y, ROWS, WIDTH), BF16),
        vm(block, BF16),
        vm((Y, Y, 8, BLOCK), F32),
        vm((Y, PAIR, BLOCK), BF16),
        vm((Y, PAIR, BLOCK), BF16),
        vm((2, ROWS, PAIR), BF16),
        vm((Y, WIDTH, PAIR), BF16),
        vm((Y, WIDTH, PAIR), BF16),
        vm((2, Z, ROWS // Z, PAIR), F32),
        vm((2, Z, ROWS // Z, PAIR), BF16),
        vm((2, Z, ROWS // Z, PAIR), BF16),
        vm((2, 2, 2, BLOCK, PAIR), F32),
        vm((2, Z // 2, 2, 2, ROWS, PAIR), BF16),
        vm((2, Z // 2, 2, 2, ROWS, PAIR), BF16),
        vm((2, 2, 2, ROWS, PAIR), BF16),
        vm((Y, 2, ROWS, PAIR), BF16),
        vm((Y, 2, ROWS, PAIR), BF16),
        vm((Y, crow, WIDTH), F32),
        vm((Y, crow, WIDTH), F32),
        vm((crow, WIDTH), F32),
        vm((crow, WIDTH), F32),
        vm((Z, crow, WIDTH), F32),
        vm((Y, crow, WIDTH), F32),
    ]
    semaphores = [
        (4,),
        (Y,),
        (4,),
        (5, Y),
        (3, Y, 2),
        (Z, 4),
        (2, Z // 2, 2, 2),
        (2, 2, 2),
        (2, Z),
        (Z,),
    ]
    for shape in semaphores:
        scratch += [dma(shape), dma(shape)]
    shapes = (
        jax.ShapeDtypeStruct(block, BF16),
        jax.ShapeDtypeStruct(block, BF16),
        jax.ShapeDtypeStruct(block, BF16),
        jax.ShapeDtypeStruct(block, BF16),
        jax.ShapeDtypeStruct((ROWS // Z, WIDTH), F32),
        jax.ShapeDtypeStruct((TAPS, WIDTH), F32),
    )
    results = pl.pallas_call(
        functools.partial(fused_kernel, Y, Z),
        out_shape=shapes,
        in_specs=[pl.BlockSpec(memory_space=pltpu.SMEM)] + [anywhere] * 6 + [vmem],
        out_specs=(anywhere,) * 6,
        scratch_shapes=scratch,
        compiler_params=pltpu.CompilerParams(
            collective_id=0, has_side_effects=True, vmem_limit_bytes=56 * 1024 * 1024
        ),
        name="conv_attention_backward",
    )(rec_lengths, query_all, key_all, value_all, cotangent, conv_input, out_proj, conv_weight)
    return pl.pallas_call(
        store_kernel, out_shape=shapes, in_specs=[vmem] * 6, out_specs=(vmem,) * 6, name="store_results"
    )(*results)


def solution(mesh):
    sizes = dict(mesh.shape)
    Y = sizes["head"]
    Z = sizes["ctx"] // (2 * Y)
    both = P("ctx", "head")
    return jax.shard_map(
        functools.partial(on_device, Y, Z),
        mesh=mesh,
        in_specs=(both, both, both, both, both, P(), P(None, "head"), P(None, "head")),
        out_specs=(both, both, both, both, both, P(None, "head")),
        check_vma=False,
    )
```
